256 devices in a mesh: group: 16 (over x, y_lo, core), blk: 16 (over z, y_hi).
Axes of the slice: x: 4, y: 4 (y_hi: 2, y_lo: 2; y = y_hi * 2 + y_lo), z: 8, core: 2. Of those that a mesh axis runs over, the one named last changes fastest.
Arguments:
- front: float32 [16, 8192, 2048], P('group', None, 'blk'), as said below
- child_blocks: float32 [16, 16, 16, 2, 128, 128], P('group', 'blk'), may hold values from -6 to 6
- child_rows: int32 [16, 16, 16, 2, 128], P('group', 'blk'), may hold values from 2048 to 8191, as said below
- child_cols: int32 [16, 16, 16, 2, 128], P('group', 'blk'), may hold values from 0 to 127, each once within a row
- child_counts: int32 [16, 16, 16], P('group', 'blk'), may hold values from 0 to 2, as said below
Outputs:
- factors: float32 [16, 8192, 2048], P('group', None, 'blk')
- pivots: float32 [16, 256], P('group')
The draws below stay inside these ranges and needn't reach their ends.
Inputs may be any that keep to these rules, and one draw needn't show every extreme that they name: Rows 0 to 2047 of each front form a symmetric matrix whose leading 2 * 128 rows and columns have a positive diagonal that dominates every row of that block; rows from 2048 on are unstructured. `child_rows`: the 128 row indices of one slot are distinct and lie at or below row 2048. `child_counts`: for every column block some destination group receives 2 live slots from every source group.
All inputs are finite; a program needn't handle non-finite values.
Results may differ from the reference program's by a relative error of at most 0.0003.
Values sent between devices are 32-bit elements; how exact they have to be, the bound alone decides.
A program may use at most 64 MiB of HBM per device.

```python
import jax
import jax.numpy as jnp
from jax import lax

BS = 128
F = 8192
PANELS = 2
CAP = 2
FRONTS = 16
BLOCKS = 16
WIN = 2048


def draw_front(key, part):
    keys = jax.random.split(key, 5)
    panel_cols = PANELS * BS
    index_ids = jnp.arange(WIN)
    in_panel = index_ids < panel_cols
    both_panel = in_panel[:, None] & in_panel[None, :]
    both_rest = (~in_panel)[:, None] & (~in_panel)[None, :]
    scales = jnp.where(both_panel, 0.9 / panel_cols, jnp.where(both_rest, 0.1, 0.2))
    upper = jax.random.uniform(keys[1], (FRONTS, WIN, WIN), jnp.float32, -1.0, 1.0)
    sym = (upper + jnp.swapaxes(upper, 1, 2)) * 0.5
    panel_diag = jax.random.uniform(keys[0], (FRONTS, WIN), jnp.float32, 1.0, 2.0)
    rest_diag = jax.random.uniform(keys[4], (FRONTS, WIN), jnp.float32, 2.0, 4.0)
    diag_values = jnp.where(in_panel[None, :], panel_diag, rest_diag)
    identity = jnp.eye(WIN, dtype=jnp.float32)
    square = sym * scales[None] * (1.0 - identity)[None] + identity[None] * diag_values[:, :, None]
    below = jax.random.normal(keys[2], (FRONTS, F - WIN, WIN), jnp.float32)
    return jnp.concatenate([square, below], axis=1).astype(jnp.float32)


def draw_child_rows(key, part):
    count = FRONTS * BLOCKS * FRONTS * CAP
    keys = jax.random.split(key, count)
    picked = jax.vmap(lambda single: jax.random.permutation(single, F - WIN)[:BS])(keys)
    return (picked + WIN).reshape(FRONTS, BLOCKS, FRONTS, CAP, BS).astype(jnp.int32)


def draw_child_counts(key, part):
    keys = jax.random.split(key, 2)
    hottest = jax.random.randint(keys[0], (BLOCKS,), 0, FRONTS)
    base = jax.random.randint(keys[1], (FRONTS, BLOCKS, FRONTS), 0, CAP + 1)
    dest = jnp.arange(FRONTS)[None, None, :]
    return jnp.where(dest == hottest[None, :, None], CAP, base).astype(jnp.int32)


def block_scale(key, shape, cuts, least, largest):
    factor_of, own = 1.0, jax.random.fold_in(key, 6)
    for position, blocks in cuts:
        draws = jnp.exp(jax.random.uniform(jax.random.fold_in(own, position), (blocks,), jnp.float32, least / len(cuts), largest / len(cuts)))
        factor_of = factor_of * jnp.repeat(draws, shape[position] // blocks).reshape([-1 if axis == position else 1 for axis in range(len(shape))])
    return factor_of


def centred(own_key, shape, spread, most, cuts=(), kind=jnp.bfloat16):
    result = jax.random.normal(own_key, shape, jnp.float32) * spread
    if len(cuts) > 0:
        result = block_scale(own_key, shape, cuts, -0.22, 0.18) * result
    return jnp.clip(result, min=-most, max=most).astype(kind)


def setup_inputs(seed: int = 0) -> dict:
    key_list = jax.random.split(jax.random.key(seed), 6)
    front = draw_front(jax.random.fold_in(key_list[5], 71), 0)
    child_blocks = centred(key_list[1], (FRONTS, BLOCKS, FRONTS, CAP, BS, BS), 1.0, 6.0, ((0, 16), (1, 16)), jnp.float32)
    child_rows = draw_child_rows(jax.random.fold_in(key_list[5], 71), 0)
    child_cols = jax.vmap(lambda own: jax.random.permutation(own, BS))(jax.random.split(key_list[3], FRONTS * BLOCKS * FRONTS * CAP)).reshape((FRONTS, BLOCKS, FRONTS, CAP, BS)).astype(jnp.int32)
    child_counts = draw_child_counts(jax.random.fold_in(key_list[5], 71), 0)
    return {"front": front, "child_blocks": child_blocks, "child_rows": child_rows, "child_cols": child_cols, "child_counts": child_counts}


def factor_panel(column, start):
    size = column.shape[1]
    square = lax.slice_in_dim(column, start, start + size, axis=0)
    lower_factor = jnp.linalg.cholesky(square)
    diag_root = jnp.diagonal(lower_factor)
    solved = lax.linalg.triangular_solve(lower_factor, column, left_side=False, lower=True, transpose_a=True)
    solved = solved / diag_root
    row_ids = lax.broadcasted_iota(jnp.int32, solved.shape, 0)
    solved = jnp.where(row_ids >= start, solved, jnp.zeros_like(solved))
    return (solved, diag_root * diag_root)

def reference(front, child_blocks, child_rows, child_cols, child_counts):

    def assemble_factor(index):
        matrix = lax.dynamic_index_in_dim(front, index, 0, False)
        blocks_here = lax.dynamic_index_in_dim(child_blocks, index, 2, False)
        row_ids = lax.dynamic_index_in_dim(child_rows, index, 2, False)
        col_local = lax.dynamic_index_in_dim(child_cols, index, 2, False)
        counts_here = lax.dynamic_index_in_dim(child_counts, index, 2, False)
        offsets = (jnp.arange(BLOCKS, dtype=jnp.int32) * BS)[None, :, None, None]
        col_ids = col_local + offsets
        live = jnp.arange(CAP, dtype=jnp.int32)[None, None, :] < counts_here[:, :, None]
        masked = jnp.where(live[..., None, None], blocks_here, jnp.zeros_like(blocks_here))
        matrix = matrix.at[row_ids[..., :, None], col_ids[..., None, :]].add(masked)
        pivot_list = []
        for panel in range(PANELS):
            start = panel * BS
            factor, pivot = factor_panel(matrix[:, start:start + BS], start)
            later = matrix[:, start + BS:] - jnp.dot(factor * pivot, factor[start + BS:WIN].T, precision=lax.Precision.HIGHEST)
            matrix = jnp.concatenate([matrix[:, :start], factor, later], axis=1)
            pivot_list.append(pivot)
        return (matrix, jnp.concatenate(pivot_list))
    factors, pivots = lax.map(assemble_factor, jnp.arange(FRONTS, dtype=jnp.int32))
    return (factors, pivots)
```

```python
import functools

import jax
import jax.numpy as jnp
from jax import lax
from jax.experimental import pallas as pl
from jax.experimental.pallas import tpu as pltpu
from jax.sharding import PartitionSpec as P

MESH = pl.DeviceIdType.MESH
F32 = jnp.float32
BF16 = jnp.bfloat16
HIGHEST = lax.Precision.HIGHEST

W = 128
TOP = 2048
EARLY = TOP // 256
TSTEP = EARLY
FIRST = TSTEP + 1
BASE = 256 * FIRST
ZR = 128
YR = 256
STEP = ZR + YR


def split(x):
    hi = x.astype(BF16)
    return hi, (x - hi.astype(F32)).astype(BF16)


def remote(src, dst, send, recv, dev):
    return pltpu.make_async_remote_copy(
        src_ref=src, dst_ref=dst, send_sem=send, recv_sem=recv,
        device_id=dev, device_id_type=MESH,
    )


def kernel(
    ngroup, nblk, rows,
    front, child, cols, idx,
    out, piv,
    mb, pan, cbuf, sbuf, rbuf, hl, xw, s_ref, x_ref,
    zz_s, zz_r, zy_s, zy_r, yy_s, yy_r, back_s, ga_s, ga_r,
    in_sem, top_sem, child_sem, out_sem,
):
    g = lax.axis_index("group")
    b = lax.axis_index("blk")
    z, yh = b // 2, b % 2
    nz = nblk // 2
    other = 1 - yh
    up = {"blk": (b + 2) % nblk}
    down = {"blk": (b + nblk - 2) % nblk}
    across = {"blk": z * 2 + other}
    nlate = (rows - TOP) // STEP
    nstep = FIRST + nlate

    get_front = pltpu.make_async_copy(front, mb, in_sem)
    get_top = pltpu.make_async_copy(
        front.at[pl.ds(0, TOP)], pan.at[yh, pl.ds(0, TOP)], top_sem
    )
    get_child = pltpu.make_async_copy(child, cbuf, child_sem)
    get_child.start()

    @pl.when(z == 0)
    def _():
        get_top.start()

    get_front.start()

    barrier = pltpu.get_barrier_semaphore()
    for i in range(1, ngroup):
        pl.semaphore_signal(
            barrier, inc=1, device_id={"group": (g + i) % ngroup}, device_id_type=MESH
        )
    for dev in (up, down, across):
        pl.semaphore_signal(barrier, inc=1, device_id=dev, device_id_type=MESH)
    pl.semaphore_wait(barrier, ngroup - 1 + 3)

    def late_row(s):
        return BASE + STEP * (s - FIRST)

    def big_z(s, d, dev):
        r = pl.ds(pl.multiple_of(256 * s + 128 * d, 128), 128)
        return remote(pan.at[:, r], pan.at[:, r], zz_s.at[d, s], zz_r.at[d, s], dev)

    def late_z(s, d, dev):
        r = pl.ds(pl.multiple_of(late_row(s) + 64 * d, 64), 64)
        return remote(pan.at[:, r], pan.at[:, r], zz_s.at[d, s], zz_r.at[d, s], dev)

    def y_rows(s, d):
        start = jnp.where(s < FIRST, 256 * s, late_row(s) + ZR) + 128 * d
        return pl.ds(pl.multiple_of(start, 128), 128)

    def own_z(s, d, dev):
        r = y_rows(s, d)
        return remote(pan.at[yh, r], pan.at[yh, r], zy_s.at[d, s], zy_r.at[d, s], dev)

    def own_y(s, d):
        r = y_rows(s, d)
        return remote(pan.at[yh, r], pan.at[yh, r], yy_s.at[d, s], yy_r.at[d, s], across)

    def from_y(s, d):
        r = y_rows(s, d)
        return remote(pan.at[other, r], pan.at[other, r], yy_s.at[d, s], yy_r.at[d, s], across)

    def back(s, d, dev):
        r = y_rows(s, d)
        return remote(pan.at[other, r], pan.at[other, r], back_s.at[s], zy_r.at[d, s], dev)

    def swap(s, start, count, k):
        r = pl.ds(pl.multiple_of(start, count), count)
        return remote(pan.at[k, r], pan.at[k, r], yy_s.at[0, s], yy_r.at[0, s], across)

    def is_big(s):
        return (s == 0) | (s == TSTEP)

    def has_y(s):
        return (s != 0) & (s != TSTEP)

    def when_step(s, fn):
        pl.when((s >= 0) & (s < nstep))(fn)

    def group_copy(t):
        return remote(sbuf.at[t], rbuf.at[g], ga_s.at[t], ga_r.at[g], {"group": t})

    def group_recv(s):
        return remote(sbuf.at[s], rbuf.at[s], ga_s.at[s], ga_r.at[s], {"group": s})

    sub = lax.broadcasted_iota(jnp.int32, (W, W), 0)
    lane = lax.broadcasted_iota(jnp.int32, (W, W), 1)
    nt = (((1,), (1,)), ((), ()))
    get_child.wait()

    @pl.loop(0, ngroup)
    def _(i):
        t = (g + 1 + i) % ngroup
        for c in range(2):
            place = (cols[t, pl.ds(c, 1), :] == sub).astype(BF16)
            hi, lo = split(cbuf[t, c])
            val = lax.dot_general(hi, place, nt, preferred_element_type=F32)
            val += lax.dot_general(lo, place, nt, preferred_element_type=F32)
            sbuf[t, pl.ds(c * W, W), :] = val
        sbuf[t, pl.ds(2 * W, 8), :] = idx[t]

        @pl.when(t != g)
        def _():
            group_copy(t).start()

    def take(s, src):
        hi, lo = split(src[s, pl.ds(0, 2 * W), :])
        r = pl.ds(pl.multiple_of(s * 2 * W, 2 * W), 2 * W)
        hl[r, pl.ds(0, W)] = hi
        hl[r, pl.ds(W, W)] = lo

    def take_children():
        take(g, sbuf)
        rbuf[g, pl.ds(2 * W, 8), :] = sbuf[g, pl.ds(2 * W, 8), :]

        @pl.loop(1, ngroup)
        def _(i):
            s = (g + ngroup - i) % ngroup
            group_recv(s).wait_recv()
            take(s, rbuf)

    PER = 4

    def extend(first):
        place = lax.broadcasted_iota(jnp.int32, (STEP, W), 0).astype(F32)
        base = first.astype(F32)

        def body(q, acc):
            parts = []
            for i in range(PER):
                for c in range(2):
                    want = rbuf[q * PER + i, pl.ds(2 * W + c, 1), :] - base
                    parts.append(jnp.where(want == place, 1.0, 0.0).astype(BF16))
            hot = jnp.concatenate(parts, axis=1)
            r = pl.ds(pl.multiple_of(q * (PER * 2 * W), PER * 2 * W), PER * 2 * W)
            got = jnp.dot(hot, hl[r, :], preferred_element_type=F32)
            return acc + (got[:, :W] + got[:, W:])

        return lax.fori_loop(0, ngroup // PER, body, jnp.zeros((STEP, W), F32))

    def product(prow, count):
        x = jnp.concatenate([pan[0, pl.ds(prow, count), :], pan[1, pl.ds(prow, count), :]], axis=1)
        hi, lo = split(x)
        got = jnp.dot(hi, xw[...], preferred_element_type=F32)
        return got[:, :W] + got[:, W:] + jnp.dot(lo, xw[:, :W], preferred_element_type=F32)

    def put(first, count, n):
        r = pl.ds(first, count)
        return pltpu.make_async_copy(mb.at[r], out.at[r], out_sem.at[n])

    def set_x(x):
        hi, lo = split(x)
        xw[:, pl.ds(0, W)] = hi
        xw[:, pl.ds(W, W)] = lo

    def pivot_rows():
        res = []
        for k in range(2):
            t = pan[k, pl.ds(256 * TSTEP + W * k, W), :]
            diag = jnp.sum(jnp.where(sub == lane, t, 0.0), axis=0, keepdims=True)
            res.append(1.0 / diag)
        return res

    def top_output():
        d0, d1 = pivot_rows()
        piv[:, pl.ds(0, W)] = d0
        piv[:, pl.ds(W, W)] = d1

        @pl.when(z == 0)
        def _():
            set_x(-pan[yh, pl.ds(256 * TSTEP, 256), :])

        @pl.when(z != 0)
        def _():
            t = jnp.concatenate(
                [pan[0, pl.ds(256 * TSTEP, 256), :], pan[1, pl.ds(256 * TSTEP, 256), :]], axis=1
            )
            d = jnp.concatenate([d0, d1], axis=1)
            v = lax.dot_general(
                t, mb[pl.ds(0, 256), :], (((0,), (0,)), ((), ())),
                precision=HIGHEST, preferred_element_type=F32,
            )
            set_x(jnp.dot(t * d, v, precision=HIGHEST, preferred_element_type=F32))

        keep = jnp.where(z == 0, 0.0, 1.0).astype(F32)

        @pl.loop(0, EARLY)
        def _(e):
            r = pl.multiple_of(e * 256, 256)
            val = mb[pl.ds(r, 256), :] * keep - product(r, 256)
            row = lax.broadcasted_iota(jnp.int32, (256, W), 0) + r
            mb[pl.ds(r, 256), :] = jnp.where((row < W) & (b == 1), 0.0, val)
            put(r, 256, e).start()

    def late_output(s, extra):
        r = pl.multiple_of(TOP + STEP * (s - FIRST), 128)
        mb[pl.ds(r, STEP), :] = extra - product(pl.multiple_of(r + 256, 128), STEP)
        put(r, STEP, EARLY + s - FIRST).start()

    def eliminate():
        x_ref[...] = (sub == lane).astype(F32)

        @pl.loop(0, W)
        def _(j):
            s, x = s_ref[...], x_ref[...]
            srow, xrow = s_ref[pl.ds(j, 1), :], x_ref[pl.ds(j, 1), :]
            d = jnp.sum(jnp.where(lane[:1] == j, srow, 0.0), axis=1, keepdims=True)
            m = jnp.sum(jnp.where(lane == j, s, 0.0), axis=1, keepdims=True)
            m = jnp.where(sub[:, :1] > j, m * (1.0 / d), 0.0)
            s_ref[...] = s - m * srow
            x_ref[...] = x - m * xrow

        d = jnp.sum(jnp.where(sub == lane, s_ref[...], 0.0), axis=0, keepdims=True)
        return jnp.transpose(x_ref[...]) * (1.0 / d)

    def factor():
        dot = functools.partial(jnp.dot, precision=HIGHEST, preferred_element_type=F32)
        base = 256 * TSTEP
        a01 = pan[1, pl.ds(0, W), :]
        s_ref[...] = pan[0, pl.ds(0, W), :]
        t00 = eliminate()
        pan[0, pl.ds(base, W), :] = t00
        pan[0, pl.ds(base + W, W), :] = jnp.zeros((W, W), F32)
        back01 = dot(t00, dot(x_ref[...], a01))
        s_ref[...] = pan[1, pl.ds(W, W), :] - lax.dot_general(
            a01, back01, (((0,), (0,)), ((), ())), precision=HIGHEST, preferred_element_type=F32
        )
        t11 = eliminate()
        pan[1, pl.ds(base + W, W), :] = t11
        pan[1, pl.ds(base, W), :] = -dot(back01, t11)

    @pl.when(z == 0)
    def _():
        get_top.wait()
        swap(0, 0, 256, yh).start()

        @pl.loop(1, EARLY)
        def _(s):
            own_z(s, 0, up).start()
            own_z(s, 1, down).start()

        swap(0, 0, 256, other).wait_recv()
        big_z(0, 0, up).start()
        big_z(0, 1, down).start()
        factor()
        big_z(TSTEP, 0, up).start()
        big_z(TSTEP, 1, down).start()
        get_front.wait()
        take_children()

        @pl.loop(0, nlate + 5)
        def _(t):
            s = t + FIRST

            @pl.when(s < nstep)
            def _():
                r = pl.multiple_of(TOP + STEP * t, 128)
                val = mb[pl.ds(r, STEP), :] + extend(r)
                pan[yh, pl.ds(pl.multiple_of(r + 256, 128), STEP), :] = val
                swap(s, late_row(s), ZR, yh).start()
                own_z(s, 0, up).start()
                own_z(s, 1, down).start()
                swap(s, late_row(s), ZR, other).wait_recv()
                late_z(s, 0, up).start()
                late_z(s, 1, down).start()

            q = s - 5

            @pl.when(q == TSTEP)
            def _():
                @pl.loop(1, EARLY)
                def _(e):
                    for d in range(2):
                        back(e, d, down).wait_recv()

                top_output()

            @pl.when(q >= FIRST)
            def _():
                for d in range(2):
                    back(q, d, down).wait_recv()
                late_output(q, 0.0)

        swap(0, 0, 256, yh).wait_send()
        for s in (0, TSTEP):
            big_z(s, 0, up).wait_send()
            big_z(s, 1, down).wait_send()

        @pl.loop(1, nstep)
        def _(s):
            @pl.when(s != TSTEP)
            def _():
                own_z(s, 0, up).wait_send()
                own_z(s, 1, down).wait_send()

            @pl.when(s >= FIRST)
            def _():
                swap(s, late_row(s), ZR, yh).wait_send()
                late_z(s, 0, up).wait_send()
                late_z(s, 1, down).wait_send()

    @pl.when(z != 0)
    def _():
        lags = (z - 1, nz - 1 - z)
        devs = (up, down)
        last = (z < nz - 1, z > 1)
        lag = jnp.maximum(lags[0], lags[1]) + 2
        get_front.wait()

        @pl.loop(0, nstep + lag)
        def _(t):
            for d in range(2):
                s = t - lags[d]

                @pl.when((s >= 0) & (s < nstep))
                def _(s=s, d=d):
                    @pl.when(is_big(s))
                    def _():
                        big_z(s, d, devs[d]).wait_recv()

                        @pl.when(last[d])
                        def _():
                            big_z(s, d, devs[d]).start()

                    @pl.when(has_y(s))
                    def _():
                        own_z(s, d, devs[d]).wait_recv()
                        own_y(s, d).start()

                        @pl.when(last[d])
                        def _():
                            own_z(s, d, devs[d]).start()

                    @pl.when(s >= FIRST)
                    def _():
                        late_z(s, d, devs[d]).wait_recv()

                        @pl.when(last[d])
                        def _():
                            late_z(s, d, devs[d]).start()

            for d in range(2):
                s = t - lags[d] - 2

                @pl.when((s >= 0) & (s < nstep) & has_y(s))
                def _(s=s, d=d):
                    from_y(s, d).wait_recv()

                    @pl.when(z == (1 if d == 0 else nz - 1))
                    def _():
                        back(s, d, devs[1 - d]).start()

            s = t - lag

            @pl.when(s == TSTEP)
            def _():
                top_output()
                take_children()

            @pl.when(s >= FIRST)
            def _():
                r = pl.multiple_of(TOP + STEP * (s - FIRST), 128)
                late_output(s, mb[pl.ds(r, STEP), :] + extend(r))

        @pl.loop(0, nstep)
        def _(s):
            for d in range(2):
                @pl.when(is_big(s) & last[d])
                def _(d=d):
                    big_z(s, d, devs[d]).wait_send()

                @pl.when(has_y(s))
                def _(d=d):
                    own_y(s, d).wait_send()

                    @pl.when(last[d])
                    def _():
                        own_z(s, d, devs[d]).wait_send()

                    @pl.when(z == (1 if d == 0 else nz - 1))
                    def _():
                        back(s, d, devs[1 - d]).wait_send()

                @pl.when((s >= FIRST) & last[d])
                def _(d=d):
                    late_z(s, d, devs[d]).wait_send()

    @pl.loop(1, ngroup)
    def _(i):
        group_copy((g + i) % ngroup).wait_send()

    @pl.loop(0, EARLY)
    def _(e):
        put(pl.multiple_of(e * 256, 256), 256, e).wait()

    @pl.loop(0, nlate)
    def _(e):
        put(pl.multiple_of(TOP + e * STEP, 128), STEP, EARLY + e).wait()


def per_device(ngroup, nblk, front, child_blocks, child_rows, child_cols, child_counts):
    rows = front.shape[1]
    slots = child_blocks.shape[3]
    nstep = FIRST + (rows - TOP) // STEP
    slot = lax.broadcasted_iota(jnp.int32, (ngroup, slots), 1)
    live = slot < child_counts.reshape(ngroup, 1)
    idx = jnp.where(live[:, :, None], child_rows[0, 0], -1).astype(F32)
    idx = jnp.pad(idx, ((0, 0), (0, 8 - slots), (0, 0)), constant_values=-1.0)
    anywhere = pl.BlockSpec(memory_space=pl.ANY)
    vmem = pl.BlockSpec(memory_space=pltpu.VMEM)
    dma = pltpu.SemaphoreType.DMA
    out, piv = pl.pallas_call(
        functools.partial(kernel, ngroup, nblk, rows),
        out_shape=(
            jax.ShapeDtypeStruct((rows, W), F32),
            jax.ShapeDtypeStruct((1, 2 * W), F32),
        ),
        in_specs=[anywhere, anywhere, vmem, vmem],
        out_specs=(anywhere, vmem),
        scratch_shapes=[
            pltpu.VMEM((rows, W), F32),
            pltpu.VMEM((2, rows + 256, W), F32),
            pltpu.VMEM((ngroup, slots, W, W), F32),
            pltpu.VMEM((ngroup, slots * W + 8, W), F32),
            pltpu.VMEM((ngroup, slots * W + 8, W), F32),
            pltpu.VMEM((ngroup * slots * W, 2 * W), BF16),
            pltpu.VMEM((2 * W, 2 * W), BF16),
            pltpu.VMEM((W, W), F32),
            pltpu.VMEM((W, W), F32),
            dma((2, nstep)), dma((2, nstep)), dma((2, nstep)), dma((2, nstep)),
            dma((2, nstep)), dma((2, nstep)), dma((nstep,)),
            dma((ngroup,)), dma((ngroup,)),
            dma, dma, dma, dma((nstep,)),
        ],
        compiler_params=pltpu.CompilerParams(
            collective_id=0, has_side_effects=True, vmem_limit_bytes=48 * 2**20
        ),
        name="extend_and_factor",
    )(front[0], child_blocks[0, 0], child_cols[0, 0], idx)
    return out[None], piv


def solution(mesh):
    in_specs = (
        P("group", None, "blk"),
        P("group", "blk", None, None, None, None),
        P("group", "blk", None, None, None),
        P("group", "blk", None, None, None),
        P("group", "blk", None),
    )
    out_specs = (P("group", None, "blk"), P("group", None))
    return jax.shard_map(
        functools.partial(per_device, mesh.shape["group"], mesh.shape["blk"]),
        mesh=mesh, in_specs=in_specs, out_specs=out_specs, check_vma=False,
    )
```

```python
import functools

import jax
import jax.numpy as jnp
from jax import lax
from jax.experimental import pallas as pl
from jax.experimental.pallas import tpu as pltpu
from jax.sharding import PartitionSpec as P

MESH = pl.DeviceIdType.MESH
F32 = jnp.float32
BF16 = jnp.bfloat16
HIGHEST = lax.Precision.HIGHEST

W = 128
TOP = 2048
EARLY = TOP // 256
TSTEP = EARLY
FIRST = TSTEP + 1
BASE = 256 * FIRST
ZR = 64
YR = 128
STEP = ZR + YR
PAIR = 2 * STEP
HOP = 3
CROSS = 3
EVERY = 4


def split(x):
    hi = x.astype(BF16)
    return hi, (x - hi.astype(F32)).astype(BF16)


def remote(src, dst, send, recv, dev):
    return pltpu.make_async_remote_copy(
        src_ref=src, dst_ref=dst, send_sem=send, recv_sem=recv,
        device_id=dev, device_id_type=MESH,
    )


def kernel(
    ngroup, nblk, rows,
    front, child, cols, idx,
    out, piv,
    mb, pan, cbuf, sbuf, rbuf, hl, xw, s_ref, x_ref,
    zz_s, zz_r, zy_s, zy_r, yy_s, yy_r, back_s, ga_s, ga_r,
    in_sem, top_sem, child_sem, out_sem,
):
    g = lax.axis_index("group")
    b = lax.axis_index("blk")
    z, yh = b // 2, b % 2
    nz = nblk // 2
    other = 1 - yh
    up = {"blk": (b + 2) % nblk}
    down = {"blk": (b + nblk - 2) % nblk}
    across = {"blk": z * 2 + other}
    nlate = (rows - TOP) // STEP
    nstep = FIRST + nlate

    get_front = pltpu.make_async_copy(front, mb, in_sem)
    get_top = pltpu.make_async_copy(
        front.at[pl.ds(0, TOP)], pan.at[yh, pl.ds(0, TOP)], top_sem
    )
    get_child = pltpu.make_async_copy(child, cbuf, child_sem)
    get_child.start()

    @pl.when(z == 0)
    def _():
        get_top.start()

    get_front.start()

    barrier = pltpu.get_barrier_semaphore()
    for i in range(1, ngroup):
        pl.semaphore_signal(
            barrier, inc=1, device_id={"group": (g + i) % ngroup}, device_id_type=MESH
        )
    for dev in (up, down, across):
        pl.semaphore_signal(barrier, inc=1, device_id=dev, device_id_type=MESH)
    pl.semaphore_wait(barrier, ngroup - 1 + 3)

    def late_row(s):
        return BASE + STEP * (s - FIRST)

    def big_z(s, d, dev):
        r = pl.ds(pl.multiple_of(256 * s + 128 * d, 128), 128)
        return remote(pan.at[:, r], pan.at[:, r], zz_s.at[d, s], zz_r.at[d, s], dev)

    def late_z(s, d, dev):
        r = pl.ds(pl.multiple_of(late_row(s) + ZR // 2 * d, ZR // 2), ZR // 2)
        return remote(pan.at[:, r], pan.at[:, r], zz_s.at[d, s], zz_r.at[d, s], dev)

    def y_rows(s, d, early):
        if early:
            return pl.ds(pl.multiple_of(256 * s + 128 * d, 128), 128)
        half = YR // 2
        return pl.ds(pl.multiple_of(late_row(s) + ZR + half * d, half), half)

    def own_z(s, d, dev, early):
        r = y_rows(s, d, early)
        return remote(pan.at[yh, r], pan.at[yh, r], zy_s.at[d, s], zy_r.at[d, s], dev)

    def own_y(s, d, early):
        r = y_rows(s, d, early)
        return remote(pan.at[yh, r], pan.at[yh, r], yy_s.at[d, s], yy_r.at[d, s], across)

    def from_y(s, d, early):
        r = y_rows(s, d, early)
        return remote(pan.at[other, r], pan.at[other, r], yy_s.at[d, s], yy_r.at[d, s], across)

    def back(s, d, dev, early):
        r = y_rows(s, d, early)
        return remote(pan.at[other, r], pan.at[other, r], back_s.at[s], zy_r.at[d, s], dev)

    def swap(s, start, count, k):
        r = pl.ds(pl.multiple_of(start, count), count)
        return remote(pan.at[k, r], pan.at[k, r], yy_s.at[0, s], yy_r.at[0, s], across)

    def is_big(s):
        return (s == 0) | (s == TSTEP)

    def is_early(s):
        return (s >= 1) & (s < TSTEP)

    def is_late(s):
        return (s >= FIRST) & (s < nstep)

    def group_copy(t):
        return remote(sbuf.at[t], rbuf.at[g], ga_s.at[t], ga_r.at[g], {"group": t})

    def group_recv(s):
        return remote(sbuf.at[s], rbuf.at[s], ga_s.at[s], ga_r.at[s], {"group": s})

    sub = lax.broadcasted_iota(jnp.int32, (W, W), 0)
    lane = lax.broadcasted_iota(jnp.int32, (W, W), 1)
    nt = (((1,), (1,)), ((), ()))

    def give(i):
        t = (g + 1 + i) % ngroup
        for c in range(2):
            place = (cols[t, pl.ds(c, 1), :] == sub).astype(BF16)
            hi, lo = split(cbuf[t, c])
            val = lax.dot_general(hi, place, nt, preferred_element_type=F32)
            val += lax.dot_general(lo, place, nt, preferred_element_type=F32)
            sbuf[t, pl.ds(c * W, W), :] = val
        sbuf[t, pl.ds(2 * W, 8), :] = idx[t]

        @pl.when(t != g)
        def _():
            group_copy(t).start()

    def take(s, src):
        hi, lo = split(src[s, pl.ds(0, 2 * W), :])
        r = pl.ds(pl.multiple_of(s * 2 * W, 2 * W), 2 * W)
        hl[r, pl.ds(0, W)] = hi
        hl[r, pl.ds(W, W)] = lo

    def take_child(i):
        s = (g + ngroup - i) % ngroup

        @pl.when(i == 0)
        def _():
            take(g, sbuf)
            rbuf[g, pl.ds(2 * W, 8), :] = sbuf[g, pl.ds(2 * W, 8), :]

        @pl.when(i > 0)
        def _():
            group_recv(s).wait_recv()
            take(s, rbuf)

    PER = 8

    def extend(first):
        place = lax.broadcasted_iota(jnp.int32, (PAIR, W), 0).astype(F32)
        base = first.astype(F32)

        def body(q, acc):
            parts = []
            for i in range(PER):
                for c in range(2):
                    want = rbuf[q * PER + i, pl.ds(2 * W + c, 1), :] - base
                    parts.append(jnp.where(want == place, 1.0, 0.0).astype(BF16))
            hot = jnp.concatenate(parts, axis=1)
            r = pl.ds(pl.multiple_of(q * (PER * 2 * W), PER * 2 * W), PER * 2 * W)
            got = jnp.dot(hot, hl[r, :], preferred_element_type=F32)
            return acc + (got[:, :W] + got[:, W:])

        return lax.fori_loop(0, ngroup // PER, body, jnp.zeros((PAIR, W), F32))

    def product(prow, count):
        x = jnp.concatenate([pan[0, pl.ds(prow, count), :], pan[1, pl.ds(prow, count), :]], axis=1)
        hi, lo = split(x)
        got = jnp.dot(hi, xw[...], preferred_element_type=F32)
        return got[:, :W] + got[:, W:] + jnp.dot(lo, xw[:, :W], preferred_element_type=F32)

    def put(first, count, n):
        r = pl.ds(first, count)
        return pltpu.make_async_copy(mb.at[r], out.at[r], out_sem.at[n])

    def set_x(x):
        hi, lo = split(x)
        xw[:, pl.ds(0, W)] = hi
        xw[:, pl.ds(W, W)] = lo

    def pivot_rows():
        res = []
        for k in range(2):
            t = pan[k, pl.ds(256 * TSTEP + W * k, W), :]
            diag = jnp.sum(jnp.where(sub == lane, t, 0.0), axis=0, keepdims=True)
            res.append(1.0 / diag)
        return res

    def top_factor():
        d0, d1 = pivot_rows()
        piv[:, pl.ds(0, W)] = d0
        piv[:, pl.ds(W, W)] = d1

        @pl.when(z == 0)
        def _():
            set_x(-pan[yh, pl.ds(256 * TSTEP, 256), :])

        @pl.when(z != 0)
        def _():
            t = jnp.concatenate(
                [pan[0, pl.ds(256 * TSTEP, 256), :], pan[1, pl.ds(256 * TSTEP, 256), :]], axis=1
            )
            d = jnp.concatenate([d0, d1], axis=1)
            v = lax.dot_general(
                t, mb[pl.ds(0, 256), :], (((0,), (0,)), ((), ())),
                precision=HIGHEST, preferred_element_type=F32,
            )
            set_x(jnp.dot(t * d, v, precision=HIGHEST, preferred_element_type=F32))

    def top_output(e):
        keep = jnp.where(z == 0, 0.0, 1.0).astype(F32)
        r = pl.multiple_of(e * 256, 256)
        val = mb[pl.ds(r, 256), :] * keep - product(r, 256)
        row = lax.broadcasted_iota(jnp.int32, (256, W), 0) + r
        mb[pl.ds(r, 256), :] = jnp.where((row < W) & (b == 1), 0.0, val)
        put(r, 256, e).start()

    def late_output(u, extra):
        r = pl.multiple_of(TOP + PAIR * u, 128)
        mb[pl.ds(r, PAIR), :] = extra - product(pl.multiple_of(r + 256, 128), PAIR)
        put(r, PAIR, EARLY + u).start()

    def eliminate():
        x_ref[...] = (sub == lane).astype(F32)

        @pl.loop(0, W)
        def _(j):
            s, x = s_ref[...], x_ref[...]
            srow, xrow = s_ref[pl.ds(j, 1), :], x_ref[pl.ds(j, 1), :]
            at = jnp.full((W, W), j, jnp.int32)
            m = jnp.take_along_axis(s, at, axis=1)
            d = jnp.take_along_axis(jnp.broadcast_to(srow, (8, W)), at[:8], axis=1)[:1]
            m = jnp.where(sub > j, m * (1.0 / d), 0.0)
            s_ref[...] = s - m * srow
            x_ref[...] = x - m * xrow

        d = jnp.sum(jnp.where(sub == lane, s_ref[...], 0.0), axis=0, keepdims=True)
        return jnp.transpose(x_ref[...]) * (1.0 / d)

    def factor():
        dot = functools.partial(jnp.dot, precision=HIGHEST, preferred_element_type=F32)
        base = 256 * TSTEP
        a01 = pan[1, pl.ds(0, W), :]
        s_ref[...] = pan[0, pl.ds(0, W), :]
        t00 = eliminate()
        pan[0, pl.ds(base, W), :] = t00
        pan[0, pl.ds(base + W, W), :] = jnp.zeros((W, W), F32)
        back01 = dot(t00, dot(x_ref[...], a01))
        s_ref[...] = pan[1, pl.ds(W, W), :] - lax.dot_general(
            a01, back01, (((0,), (0,)), ((), ())), precision=HIGHEST, preferred_element_type=F32
        )
        t11 = eliminate()
        pan[1, pl.ds(base + W, W), :] = t11
        pan[1, pl.ds(base, W), :] = -dot(back01, t11)

    @pl.when(z == 0)
    def _():
        get_top.wait()
        swap(0, 0, 256, yh).start()
        get_child.wait()

        @pl.loop(0, ngroup)
        def _(i):
            give(i)

            @pl.when(i == 3)
            def _():
                swap(0, 0, 256, other).wait_recv()
                big_z(0, 0, up).start()
                big_z(0, 1, down).start()

            @pl.when((i > 3) & (i < 3 + EARLY))
            def _():
                own_z(i - 3, 0, up, True).start()
                own_z(i - 3, 1, down, True).start()

        factor()
        big_z(TSTEP, 0, up).start()
        big_z(TSTEP, 1, down).start()
        get_front.wait()
        pl.loop(0, ngroup)(take_child)

        def own_send(s):
            swap(s, late_row(s), ZR, yh).start()
            own_z(s, 0, up, False).start()
            own_z(s, 1, down, False).start()

        def both_send(s):
            swap(s, late_row(s), ZR, other).wait_recv()
            late_z(s, 0, up).start()
            late_z(s, 1, down).start()

        @pl.loop(0, nlate // 2)
        def _(u):
            r = pl.multiple_of(TOP + PAIR * u, 128)
            val = mb[pl.ds(r, PAIR), :] + extend(r)
            pan[yh, pl.ds(pl.multiple_of(r + 256, 128), PAIR), :] = val
            s = FIRST + 2 * u
            own_send(s)
            own_send(s + 1)

            @pl.when(u > 0)
            def _():
                both_send(s - 2)
                both_send(s - 1)

        both_send(nstep - 2)
        both_send(nstep - 1)
        top_factor()
        top_output(0)

        @pl.loop(0, nlate // 2)
        def _(u):
            for i in range(2):
                for d in range(2):
                    back(FIRST + 2 * u + i, d, down, False).wait_recv()
            late_output(u, 0.0)

        @pl.loop(1, EARLY)
        def _(e):
            for d in range(2):
                back(e, d, down, True).wait_recv()
            top_output(e)

        swap(0, 0, 256, yh).wait_send()
        for s in (0, TSTEP):
            big_z(s, 0, up).wait_send()
            big_z(s, 1, down).wait_send()

        @pl.loop(1, EARLY)
        def _(s):
            own_z(s, 0, up, True).wait_send()
            own_z(s, 1, down, True).wait_send()

        @pl.loop(FIRST, nstep)
        def _(s):
            own_z(s, 0, up, False).wait_send()
            own_z(s, 1, down, False).wait_send()
            swap(s, late_row(s), ZR, yh).wait_send()
            late_z(s, 0, up).wait_send()
            late_z(s, 1, down).wait_send()

    @pl.when(z != 0)
    def _():
        lags = (HOP * (z - 1), HOP * (nz - 1 - z))
        devs = (up, down)
        last = (z < nz - 1, z > 1)
        turn = (z == 1, z == nz - 1)
        lag = HOP * (nz - 2) + CROSS
        get_child.wait()
        pl.loop(0, ngroup)(give)
        get_front.wait()

        def crossing(s):
            n = s - FIRST
            return jnp.where((n > 0) & (n % EVERY == 0) & (n < EVERY * EARLY), n // EVERY, 0)

        @pl.loop(0, nstep + lag)
        def _(t):
            for d in range(2):
                s = t - lags[d]
                e = crossing(s)

                @pl.when(is_big(s))
                def _(s=s, d=d):
                    big_z(s, d, devs[d]).wait_recv()

                    @pl.when(last[d])
                    def _():
                        big_z(s, d, devs[d]).start()

                for early, cond in ((True, is_early(s)), (False, is_late(s))):
                    @pl.when(cond)
                    def _(s=s, d=d, early=early):
                        own_z(s, d, devs[d], early).wait_recv()

                        @pl.when(last[d])
                        def _():
                            own_z(s, d, devs[d], early).start()

                        if not early:
                            own_y(s, d, early).start()

                @pl.when(e > 0)
                def _(e=e, d=d):
                    own_y(e, d, True).start()

            for d in range(2):
                s = t - lags[d] - CROSS
                e = crossing(s)

                @pl.when(is_late(s))
                def _(s=s, d=d):
                    late_z(s, d, devs[d]).wait_recv()

                    @pl.when(last[d])
                    def _():
                        late_z(s, d, devs[d]).start()

                for early, q, cond in ((False, s, is_late(s)), (True, e, e > 0)):
                    @pl.when(cond)
                    def _(q=q, d=d, early=early):
                        from_y(q, d, early).wait_recv()

                        @pl.when(turn[d])
                        def _():
                            back(q, d, devs[1 - d], early).start()

            s = t - lag
            n = s - FIRST

            @pl.when((n >= -8) & (n < 0))
            def _():
                take_child(2 * (n + 8))
                take_child(2 * (n + 8) + 1)

            @pl.when(s == TSTEP)
            def _():
                top_factor()
                top_output(0)

            @pl.when(crossing(s) > 0)
            def _():
                top_output(crossing(s))

            @pl.when((n > 0) & (n % 2 == 1))
            def _():
                u = n // 2
                r = pl.multiple_of(TOP + PAIR * u, 128)
                late_output(u, mb[pl.ds(r, PAIR), :] + extend(r))

        for s in (0, TSTEP):
            for d in range(2):
                @pl.when(last[d])
                def _(s=s, d=d):
                    big_z(s, d, devs[d]).wait_send()

        def drain(s, early):
            for d in range(2):
                own_y(s, d, early).wait_send()

                @pl.when(last[d])
                def _(d=d):
                    own_z(s, d, devs[d], early).wait_send()
                    if not early:
                        late_z(s, d, devs[d]).wait_send()

                @pl.when(turn[d])
                def _(d=d):
                    back(s, d, devs[1 - d], early).wait_send()

        pl.loop(1, EARLY)(lambda s: drain(s, True))
        pl.loop(FIRST, nstep)(lambda s: drain(s, False))

    @pl.loop(1, ngroup)
    def _(i):
        group_copy((g + i) % ngroup).wait_send()

    @pl.loop(0, EARLY)
    def _(e):
        put(pl.multiple_of(e * 256, 256), 256, e).wait()

    @pl.loop(0, nlate // 2)
    def _(u):
        put(pl.multiple_of(TOP + u * PAIR, 128), PAIR, EARLY + u).wait()


def per_device(ngroup, nblk, front, child_blocks, child_rows, child_cols, child_counts):
    rows = front.shape[1]
    slots = child_blocks.shape[3]
    nstep = FIRST + (rows - TOP) // STEP
    slot = lax.broadcasted_iota(jnp.int32, (ngroup, slots), 1)
    live = slot < child_counts.reshape(ngroup, 1)
    idx = jnp.where(live[:, :, None], child_rows[0, 0], -1).astype(F32)
    idx = jnp.pad(idx, ((0, 0), (0, 8 - slots), (0, 0)), constant_values=-1.0)
    anywhere = pl.BlockSpec(memory_space=pl.ANY)
    vmem = pl.BlockSpec(memory_space=pltpu.VMEM)
    dma = pltpu.SemaphoreType.DMA
    out, piv = pl.pallas_call(
        functools.partial(kernel, ngroup, nblk, rows),
        out_shape=(
            jax.ShapeDtypeStruct((rows, W), F32),
            jax.ShapeDtypeStruct((1, 2 * W), F32),
        ),
        in_specs=[anywhere, anywhere, vmem, vmem],
        out_specs=(anywhere, vmem),
        scratch_shapes=[
            pltpu.VMEM((rows, W), F32),
            pltpu.VMEM((2, rows + 256, W), F32),
            pltpu.VMEM((ngroup, slots, W, W), F32),
            pltpu.VMEM((ngroup, slots * W + 8, W), F32),
            pltpu.VMEM((ngroup, slots * W + 8, W), F32),
            pltpu.VMEM((ngroup * slots * W, 2 * W), BF16),
            pltpu.VMEM((2 * W, 2 * W), BF16),
            pltpu.VMEM((W, W), F32),
            pltpu.VMEM((W, W), F32),
            dma((2, nstep)), dma((2, nstep)), dma((2, nstep)), dma((2, nstep)),
            dma((2, nstep)), dma((2, nstep)), dma((nstep,)),
            dma((ngroup,)), dma((ngroup,)),
            dma, dma, dma, dma((nstep,)),
        ],
        compiler_params=pltpu.CompilerParams(
            collective_id=0, has_side_effects=True, vmem_limit_bytes=48 * 2**20
        ),
        name="extend_and_factor",
    )(front[0], child_blocks[0, 0], child_cols[0, 0], idx)
    return out[None], piv


def solution(mesh):
    in_specs = (
        P("group", None, "blk"),
        P("group", "blk", None, None, None, None),
        P("group", "blk", None, None, None),
        P("group", "blk", None, None, None),
        P("group", "blk", None),
    )
    out_specs = (P("group", None, "blk"), P("group", None))
    return jax.shard_map(
        functools.partial(per_device, mesh.shape["group"], mesh.shape["blk"]),
        mesh=mesh, in_specs=in_specs, out_specs=out_specs, check_vma=False,
    )
```

```python
import functools

import jax
import jax.numpy as jnp
from jax import lax
from jax.experimental import pallas as pl
from jax.experimental.pallas import tpu as pltpu
from jax.sharding import PartitionSpec as P

MESH = pl.DeviceIdType.MESH
F32 = jnp.float32
BF16 = jnp.bfloat16
HIGHEST = lax.Precision.HIGHEST

W = 128
TOP = 2048
EARLY = TOP // 256
TSTEP = EARLY
FIRST = TSTEP + 1
BASE = 256 * FIRST
ZR = 64
YR = 128
STEP = ZR + YR
PAIR = 2 * STEP
HOP = 3
CROSS = 3
EVERY = 4


def split(x):
    hi = x.astype(BF16)
    return hi, (x - hi.astype(F32)).astype(BF16)


def remote(src, dst, send, recv, dev):
    return pltpu.make_async_remote_copy(
        src_ref=src, dst_ref=dst, send_sem=send, recv_sem=recv,
        device_id=dev, device_id_type=MESH,
    )


def kernel(
    ngroup, nblk, rows,
    front, child, child_rows, cols, counts,
    out, piv,
    mb, pan, sbuf, rbuf, hl, xw, s_ref, x_ref,
    zz_s, zz_r, zy_s, zy_r, yy_s, yy_r, back_s, ga_s, ga_r,
    in_sem, top_sem, child_sem, out_sem,
):
    g = lax.axis_index("group")
    b = lax.axis_index("blk")
    z, yh = b // 2, b % 2
    nz = nblk // 2
    other = 1 - yh
    up = {"blk": (b + 2) % nblk}
    down = {"blk": (b + nblk - 2) % nblk}
    across = {"blk": z * 2 + other}
    nlate = (rows - TOP) // STEP
    nstep = FIRST + nlate

    get_front = pltpu.make_async_copy(front, mb, in_sem)
    get_top = pltpu.make_async_copy(
        front.at[pl.ds(0, TOP)], pan.at[yh, pl.ds(0, TOP)], top_sem
    )
    get_child = pltpu.make_async_copy(child, sbuf.at[:, pl.ds(0, 2 * W)], child_sem)
    get_child.start()

    @pl.when(z == 0)
    def _():
        get_top.start()

    get_front.start()

    @pl.loop(0, ngroup)
    def _(t):
        slot = lax.broadcasted_iota(jnp.int32, (2, W), 0)
        at = jnp.where(slot < counts[0, t], child_rows[t], -1)
        sbuf[t, pl.ds(2 * W, 2), :] = at.astype(F32)
        sbuf[t, pl.ds(2 * W + 2, 2), :] = cols[t].astype(F32)

    barrier = pltpu.get_barrier_semaphore()
    for i in range(1, ngroup):
        pl.semaphore_signal(
            barrier, inc=1, device_id={"group": (g + i) % ngroup}, device_id_type=MESH
        )
    for dev in (up, down, across):
        pl.semaphore_signal(barrier, inc=1, device_id=dev, device_id_type=MESH)
    pl.semaphore_wait(barrier, ngroup - 1 + 3)

    def late_row(s):
        return BASE + STEP * (s - FIRST)

    def big_z(s, d, dev):
        r = pl.ds(pl.multiple_of(256 * s + 128 * d, 128), 128)
        return remote(pan.at[:, r], pan.at[:, r], zz_s.at[d], zz_r.at[d, s], dev)

    def late_z(s, d, dev):
        r = pl.ds(pl.multiple_of(late_row(s) + ZR // 2 * d, ZR // 2), ZR // 2)
        return remote(pan.at[:, r], pan.at[:, r], zz_s.at[d], zz_r.at[d, s], dev)

    def y_rows(s, d, early):
        if early:
            return pl.ds(pl.multiple_of(256 * s + 128 * d, 128), 128)
        half = YR // 2
        return pl.ds(pl.multiple_of(late_row(s) + ZR + half * d, half), half)

    def own_z(s, d, dev, early):
        r = y_rows(s, d, early)
        return remote(pan.at[yh, r], pan.at[yh, r], zy_s.at[d], zy_r.at[d, s], dev)

    def own_y(s, d, early):
        r = y_rows(s, d, early)
        return remote(pan.at[yh, r], pan.at[yh, r], yy_s.at[d], yy_r.at[d, s], across)

    def from_y(s, d, early):
        r = y_rows(s, d, early)
        return remote(pan.at[other, r], pan.at[other, r], yy_s.at[d], yy_r.at[d, s], across)

    def back(s, d, dev, early):
        r = y_rows(s, d, early)
        return remote(pan.at[other, r], pan.at[other, r], back_s, zy_r.at[d, s], dev)

    def swap(s, start, count, k):
        r = pl.ds(pl.multiple_of(start, count), count)
        return remote(pan.at[k, r], pan.at[k, r], yy_s.at[0], yy_r.at[0, s], across)

    own_rows = (EARLY - 1) * W + nlate * (YR // 2)

    def sent_z(d):
        dev = (up, down)[d]
        own = pan.at[yh, pl.ds(0, own_rows)]
        remote(own, own, zy_s.at[d], zy_r.at[d, 0], dev).wait_send()
        both = pan.at[:, pl.ds(0, 2 * W + nlate * (ZR // 2))]
        remote(both, both, zz_s.at[d], zz_r.at[d, 0], dev).wait_send()

    def is_big(s):
        return (s == 0) | (s == TSTEP)

    def is_early(s):
        return (s >= 1) & (s < TSTEP)

    def is_late(s):
        return (s >= FIRST) & (s < nstep)

    def group_copy(t):
        return remote(sbuf.at[t], rbuf.at[g], ga_s, ga_r.at[g], {"group": t})

    def group_recv(s):
        return remote(sbuf.at[s], rbuf.at[s], ga_s, ga_r.at[s], {"group": s})

    sub = lax.broadcasted_iota(jnp.int32, (W, W), 0)
    lane = lax.broadcasted_iota(jnp.int32, (W, W), 1)
    nt = (((1,), (1,)), ((), ()))

    def give(i):
        t = (g + 1 + i) % ngroup

        @pl.when(t != g)
        def _():
            group_copy(t).start()

    def take(s, src):
        for c in range(2):
            place = (src[s, pl.ds(2 * W + 2 + c, 1), :] == sub.astype(F32)).astype(BF16)
            both = jnp.concatenate(split(src[s, pl.ds(c * W, W), :]), axis=0)
            got = lax.dot_general(both, place, nt, preferred_element_type=F32).astype(BF16)
            r = pl.ds(pl.multiple_of(s * 2 * W + c * W, W), W)
            hl[r, pl.ds(0, W)] = got[:W]
            hl[r, pl.ds(W, W)] = got[W:]

    def take_child(i):
        s = (g + ngroup - i) % ngroup

        @pl.when(i == 0)
        def _():
            take(g, sbuf)
            rbuf[g, pl.ds(2 * W, 8), :] = sbuf[g, pl.ds(2 * W, 8), :]

        @pl.when(i > 0)
        def _():
            group_recv(s).wait_recv()
            take(s, rbuf)

    PER = 8

    def extend(first):
        place = lax.broadcasted_iota(jnp.int32, (PAIR, W), 0).astype(F32)
        base = first.astype(F32)

        def body(q, acc):
            parts = []
            for i in range(PER):
                for c in range(2):
                    want = rbuf[q * PER + i, pl.ds(2 * W + c, 1), :] - base
                    parts.append(jnp.where(want == place, 1.0, 0.0).astype(BF16))
            hot = jnp.concatenate(parts, axis=1)
            r = pl.ds(pl.multiple_of(q * (PER * 2 * W), PER * 2 * W), PER * 2 * W)
            got = jnp.dot(hot, hl[r, :], preferred_element_type=F32)
            return acc + (got[:, :W] + got[:, W:])

        return lax.fori_loop(0, ngroup // PER, body, jnp.zeros((PAIR, W), F32))

    def product(prow, count):
        x = jnp.concatenate([pan[0, pl.ds(prow, count), :], pan[1, pl.ds(prow, count), :]], axis=1)
        hi, lo = split(x)
        got = jnp.dot(hi, xw[...], preferred_element_type=F32)
        return got[:, :W] + got[:, W:] + jnp.dot(lo, xw[:, :W], preferred_element_type=F32)

    def put(first, count, n):
        r = pl.ds(first, count)
        return pltpu.make_async_copy(mb.at[r], out.at[r], out_sem.at[n])

    def set_x(x):
        hi, lo = split(x)
        xw[:, pl.ds(0, W)] = hi
        xw[:, pl.ds(W, W)] = lo

    def pivot_rows():
        res = []
        for k in range(2):
            t = pan[k, pl.ds(256 * TSTEP + W * k, W), :]
            diag = jnp.sum(jnp.where(sub == lane, t, 0.0), axis=0, keepdims=True)
            res.append(1.0 / diag)
        return res

    def top_factor():
        d0, d1 = pivot_rows()
        piv[:, pl.ds(0, W)] = d0
        piv[:, pl.ds(W, W)] = d1

        @pl.when(z == 0)
        def _():
            set_x(-pan[yh, pl.ds(256 * TSTEP, 256), :])

        @pl.when(z != 0)
        def _():
            t = jnp.concatenate(
                [pan[0, pl.ds(256 * TSTEP, 256), :], pan[1, pl.ds(256 * TSTEP, 256), :]], axis=1
            )
            d = jnp.concatenate([d0, d1], axis=1)
            v = lax.dot_general(
                t, mb[pl.ds(0, 256), :], (((0,), (0,)), ((), ())),
                precision=HIGHEST, preferred_element_type=F32,
            )
            set_x(jnp.dot(t * d, v, precision=HIGHEST, preferred_element_type=F32))

    def top_output(e):
        keep = jnp.where(z == 0, 0.0, 1.0).astype(F32)
        r = pl.multiple_of(e * 256, 256)
        val = mb[pl.ds(r, 256), :] * keep - product(r, 256)
        row = lax.broadcasted_iota(jnp.int32, (256, W), 0) + r
        mb[pl.ds(r, 256), :] = jnp.where((row < W) & (b == 1), 0.0, val)
        put(r, 256, e).start()

    def late_output(u, extra):
        r = pl.multiple_of(TOP + PAIR * u, 128)
        mb[pl.ds(r, PAIR), :] = extra - product(pl.multiple_of(r + 256, 128), PAIR)
        put(r, PAIR, EARLY + u).start()

    def eliminate():
        x_ref[...] = (sub == lane).astype(F32)

        for lo in range(0, W, 32):
            rest = pl.ds(lo, W - lo)

            @pl.loop(lo, lo + 32)
            def _(j):
                s, x = s_ref[rest, :], x_ref[rest, :]
                srow, xrow = s_ref[pl.ds(j, 1), :], x_ref[pl.ds(j, 1), :]
                at = jnp.full((W - lo, W), j, jnp.int32)
                m = jnp.take_along_axis(s, at, axis=1)
                d = jnp.take_along_axis(jnp.broadcast_to(srow, (8, W)), at[:8], axis=1)[:1]
                m = jnp.where(sub[lo:] > j, m * (1.0 / d), 0.0)
                s_ref[rest, :] = s - m * srow
                x_ref[rest, :] = x - m * xrow

        d = jnp.sum(jnp.where(sub == lane, s_ref[...], 0.0), axis=0, keepdims=True)
        return jnp.transpose(x_ref[...]) * (1.0 / d)

    def factor():
        dot = functools.partial(jnp.dot, precision=HIGHEST, preferred_element_type=F32)
        base = 256 * TSTEP
        a01 = pan[1, pl.ds(0, W), :]
        s_ref[...] = pan[0, pl.ds(0, W), :]
        t00 = eliminate()
        pan[0, pl.ds(base, W), :] = t00
        pan[0, pl.ds(base + W, W), :] = jnp.zeros((W, W), F32)
        back01 = dot(t00, dot(x_ref[...], a01))
        s_ref[...] = pan[1, pl.ds(W, W), :] - lax.dot_general(
            a01, back01, (((0,), (0,)), ((), ())), precision=HIGHEST, preferred_element_type=F32
        )
        t11 = eliminate()
        pan[1, pl.ds(base + W, W), :] = t11
        pan[1, pl.ds(base, W), :] = -dot(back01, t11)

    @pl.when(z == 0)
    def _():
        get_top.wait()
        swap(0, 0, 256, yh).start()
        get_child.wait()

        @pl.loop(0, ngroup)
        def _(i):
            give(i)

            @pl.when(i == 3)
            def _():
                swap(0, 0, 256, other).wait_recv()
                big_z(0, 0, up).start()
                big_z(0, 1, down).start()

            @pl.when((i > 3) & (i < 3 + EARLY))
            def _():
                own_z(i - 3, 0, up, True).start()
                own_z(i - 3, 1, down, True).start()

        factor()
        big_z(TSTEP, 0, up).start()
        big_z(TSTEP, 1, down).start()
        get_front.wait()
        pl.loop(0, ngroup)(take_child)

        def own_send(s):
            swap(s, late_row(s), ZR, yh).start()
            own_z(s, 0, up, False).start()
            own_z(s, 1, down, False).start()

        def both_send(s):
            swap(s, late_row(s), ZR, other).wait_recv()
            late_z(s, 0, up).start()
            late_z(s, 1, down).start()

        @pl.loop(0, nlate // 2)
        def _(u):
            r = pl.multiple_of(TOP + PAIR * u, 128)
            val = mb[pl.ds(r, PAIR), :] + extend(r)
            pan[yh, pl.ds(pl.multiple_of(r + 256, 128), PAIR), :] = val
            s = FIRST + 2 * u
            own_send(s)
            own_send(s + 1)

            @pl.when(u > 0)
            def _():
                both_send(s - 2)
                both_send(s - 1)

        both_send(nstep - 2)
        both_send(nstep - 1)
        top_factor()
        top_output(0)

        @pl.loop(0, nlate // 2)
        def _(u):
            for i in range(2):
                for d in range(2):
                    back(FIRST + 2 * u + i, d, down, False).wait_recv()
            late_output(u, 0.0)

        @pl.loop(1, EARLY)
        def _(e):
            for d in range(2):
                back(e, d, down, True).wait_recv()
            top_output(e)

        swapped = pan.at[yh, pl.ds(0, 256 + nlate * ZR)]
        remote(swapped, swapped, yy_s.at[0], yy_r.at[0, 0], across).wait_send()
        for d in range(2):
            sent_z(d)

    @pl.when(z != 0)
    def _():
        lags = (HOP * (z - 1), HOP * (nz - 1 - z))
        devs = (up, down)
        last = (z < nz - 1, z > 1)
        turn = (z == 1, z == nz - 1)
        lag = HOP * (nz - 2) + CROSS
        get_child.wait()
        pl.loop(0, ngroup)(give)
        get_front.wait()

        def crossing(s):
            n = s - FIRST
            return jnp.where((n > 0) & (n % EVERY == 0) & (n < EVERY * EARLY), n // EVERY, 0)

        @pl.loop(0, nstep + lag)
        def _(t):
            for d in range(2):
                s = t - lags[d]

                @pl.when(is_big(s))
                def _(s=s, d=d):
                    big_z(s, d, devs[d]).wait_recv()

                    @pl.when(last[d])
                    def _():
                        big_z(s, d, devs[d]).start()

                for early, cond in ((True, is_early(s)), (False, is_late(s))):
                    @pl.when(cond)
                    def _(s=s, d=d, early=early):
                        own_z(s, d, devs[d], early).wait_recv()

                        @pl.when(last[d])
                        def _():
                            own_z(s, d, devs[d], early).start()

                        own_y(s, d, early).start()

            for d in range(2):
                s = t - lags[d] - CROSS
                e = crossing(s)

                @pl.when(is_late(s))
                def _(s=s, d=d):
                    late_z(s, d, devs[d]).wait_recv()

                    @pl.when(last[d])
                    def _():
                        late_z(s, d, devs[d]).start()

                for early, q, cond in ((False, s, is_late(s)), (True, e, e > 0)):
                    @pl.when(cond)
                    def _(q=q, d=d, early=early):
                        from_y(q, d, early).wait_recv()

                        @pl.when(turn[d])
                        def _():
                            back(q, d, devs[1 - d], early).start()

            s = t - lag
            n = s - FIRST

            @pl.when((n >= -8) & (n < 0))
            def _():
                take_child(2 * (n + 8))
                take_child(2 * (n + 8) + 1)

            @pl.when(s == TSTEP)
            def _():
                top_factor()
                top_output(0)

            @pl.when(crossing(s) > 0)
            def _():
                top_output(crossing(s))

            @pl.when((n > 0) & (n % 2 == 1))
            def _():
                u = n // 2
                r = pl.multiple_of(TOP + PAIR * u, 128)
                late_output(u, mb[pl.ds(r, PAIR), :] + extend(r))

        for d in range(2):
            own = pan.at[yh, pl.ds(0, own_rows)]
            remote(own, own, yy_s.at[d], yy_r.at[d, 0], across).wait_send()
            pl.when(last[d])(functools.partial(sent_z, d))

        @pl.when((z == 1) | (z == nz - 1))
        def _():
            own = pan.at[yh, pl.ds(0, own_rows)]
            remote(own, own, back_s, zy_r.at[0, 0], up).wait_send()

    given = sbuf.at[pl.ds(0, ngroup - 1)]
    remote(given, given, ga_s, ga_r.at[0], {"group": (g + 1) % ngroup}).wait_send()

    @pl.loop(0, EARLY)
    def _(e):
        put(pl.multiple_of(e * 256, 256), 256, e).wait()

    @pl.loop(0, nlate // 2)
    def _(u):
        put(pl.multiple_of(TOP + u * PAIR, 128), PAIR, EARLY + u).wait()


def per_device(ngroup, nblk, front, child_blocks, child_rows, child_cols, child_counts):
    rows = front.shape[1]
    slots = child_blocks.shape[3]
    nstep = FIRST + (rows - TOP) // STEP
    hbm = pl.BlockSpec(memory_space=pltpu.HBM)
    vmem = pl.BlockSpec(memory_space=pltpu.VMEM)
    smem = pl.BlockSpec(memory_space=pltpu.SMEM)
    dma = pltpu.SemaphoreType.DMA
    out, piv = pl.pallas_call(
        functools.partial(kernel, ngroup, nblk, rows),
        out_shape=(
            jax.ShapeDtypeStruct((rows, W), F32),
            jax.ShapeDtypeStruct((1, 2 * W), F32),
        ),
        in_specs=[hbm, hbm, vmem, vmem, smem],
        out_specs=(hbm, vmem),
        scratch_shapes=[
            pltpu.VMEM((rows, W), F32),
            pltpu.VMEM((2, rows + 256, W), F32),
            pltpu.VMEM((ngroup, slots * W + 8, W), F32),
            pltpu.VMEM((ngroup, slots * W + 8, W), F32),
            pltpu.VMEM((ngroup * slots * W, 2 * W), BF16),
            pltpu.VMEM((2 * W, 2 * W), BF16),
            pltpu.VMEM((W, W), F32),
            pltpu.VMEM((W, W), F32),
            dma((2,)), dma((2, nstep)), dma((2,)), dma((2, nstep)),
            dma((2,)), dma((2, nstep)), dma,
            dma, dma((ngroup,)),
            dma, dma, dma, dma((nstep,)),
        ],
        compiler_params=pltpu.CompilerParams(
            collective_id=0, has_side_effects=True, vmem_limit_bytes=56 * 2**20
        ),
        name="extend_and_factor",
    )(
        front[0], child_blocks.reshape(ngroup, slots * W, W), child_rows[0, 0],
        child_cols[0, 0], child_counts.reshape(1, ngroup),
    )
    return out[None], piv


def solution(mesh):
    in_specs = (
        P("group", None, "blk"),
        P("group", "blk", None, None, None, None),
        P("group", "blk", None, None, None),
        P("group", "blk", None, None, None),
        P("group", "blk", None),
    )
    out_specs = (P("group", None, "blk"), P("group", None))
    return jax.shard_map(
        functools.partial(per_device, mesh.shape["group"], mesh.shape["blk"]),
        mesh=mesh, in_specs=in_specs, out_specs=out_specs, check_vma=False,
    )
```

```python
import functools

import jax
import jax.numpy as jnp
from jax import lax
from jax.experimental import pallas as pl
from jax.experimental.pallas import tpu as pltpu
from jax.sharding import PartitionSpec as P

MESH = pl.DeviceIdType.MESH
F32 = jnp.float32
BF16 = jnp.bfloat16
HIGHEST = lax.Precision.HIGHEST

W = 128
TOP = 2048
EARLY = TOP // 256
TSTEP = EARLY
FIRST = TSTEP + 1
BASE = 256 * FIRST
ZR = 64
YR = 128
STEP = ZR + YR
PAIR = 2 * STEP
HOP = 3
CROSS = 4
EVERY = 4


def split(x):
    hi = x.astype(BF16)
    return hi, (x - hi.astype(F32)).astype(BF16)


def remote(src, dst, send, recv, dev):
    return pltpu.make_async_remote_copy(
        src_ref=src, dst_ref=dst, send_sem=send, recv_sem=recv,
        device_id=dev, device_id_type=MESH,
    )


def kernel(
    ngroup, nblk, rows,
    front, child, child_rows, cols, counts,
    out, piv,
    mb, pan, sbuf, rbuf, hl, xw, s_ref, x_ref,
    zz_s, zz_r, zy_s, zy_r, yy_s, yy_r, back_s, ga_s, ga_r,
    in_sem, top_sem, child_sem, out_sem,
):
    g = lax.axis_index("group")
    b = lax.axis_index("blk")
    z, yh = b // 2, b % 2
    nz = nblk // 2
    other = 1 - yh
    up = {"blk": (b + 2) % nblk}
    down = {"blk": (b + nblk - 2) % nblk}
    across = {"blk": z * 2 + other}
    nlate = (rows - TOP) // STEP
    nstep = FIRST + nlate

    get_front = pltpu.make_async_copy(front, mb, in_sem)
    get_top = pltpu.make_async_copy(
        front.at[pl.ds(0, TOP)], pan.at[yh, pl.ds(0, TOP)], top_sem
    )
    get_child = pltpu.make_async_copy(child, sbuf.at[:, pl.ds(0, 2 * W)], child_sem)
    get_child.start()

    @pl.when(z == 0)
    def _():
        get_top.start()

    get_front.start()

    @pl.loop(0, ngroup)
    def _(t):
        slot = lax.broadcasted_iota(jnp.int32, (2, W), 0)
        at = jnp.where(slot < counts[0, t], child_rows[t], -1)
        sbuf[t, pl.ds(2 * W, 2), :] = at.astype(F32)
        sbuf[t, pl.ds(2 * W + 2, 2), :] = cols[t].astype(F32)

    barrier = pltpu.get_barrier_semaphore()
    for i in range(1, ngroup):
        pl.semaphore_signal(
            barrier, inc=1, device_id={"group": (g + i) % ngroup}, device_id_type=MESH
        )
    for dev in (up, down, across):
        pl.semaphore_signal(barrier, inc=1, device_id=dev, device_id_type=MESH)
    pl.semaphore_wait(barrier, ngroup - 1 + 3)

    def late_row(s):
        return BASE + STEP * (s - FIRST)

    def big_z(s, d, dev):
        r = pl.ds(pl.multiple_of(256 * s + 128 * d, 128), 128)
        return remote(pan.at[:, r], pan.at[:, r], zz_s.at[d], zz_r.at[d, s], dev)

    def late_z(s, d, dev):
        r = pl.ds(pl.multiple_of(late_row(s) + ZR // 2 * d, ZR // 2), ZR // 2)
        return remote(pan.at[:, r], pan.at[:, r], zz_s.at[d], zz_r.at[d, s], dev)

    def y_rows(s, d, early):
        if early:
            return pl.ds(pl.multiple_of(256 * s + 128 * d, 128), 128)
        half = YR // 2
        return pl.ds(pl.multiple_of(late_row(s) + ZR + half * d, half), half)

    def own_z(s, d, dev, early):
        r = y_rows(s, d, early)
        return remote(pan.at[yh, r], pan.at[yh, r], zy_s.at[d], zy_r.at[d, s], dev)

    def own_y(s, d, early):
        r = y_rows(s, d, early)
        return remote(pan.at[yh, r], pan.at[yh, r], yy_s.at[d], yy_r.at[d, s], across)

    def from_y(s, d, early):
        r = y_rows(s, d, early)
        return remote(pan.at[other, r], pan.at[other, r], yy_s.at[d], yy_r.at[d, s], across)

    def back(s, d, dev, early):
        r = y_rows(s, d, early)
        return remote(pan.at[other, r], pan.at[other, r], back_s, zy_r.at[d, s], dev)

    def swap(s, start, count, k):
        r = pl.ds(pl.multiple_of(start, count), count)
        return remote(pan.at[k, r], pan.at[k, r], yy_s.at[0], yy_r.at[0, s], across)

    own_rows = (EARLY - 1) * W + nlate * (YR // 2)

    def sent_z(d):
        dev = (up, down)[d]
        own = pan.at[yh, pl.ds(0, own_rows)]
        remote(own, own, zy_s.at[d], zy_r.at[d, 0], dev).wait_send()
        both = pan.at[:, pl.ds(0, 2 * W + nlate * (ZR // 2))]
        remote(both, both, zz_s.at[d], zz_r.at[d, 0], dev).wait_send()

    def is_big(s):
        return (s == 0) | (s == TSTEP)

    def is_early(s):
        return (s >= 1) & (s < TSTEP)

    def is_late(s):
        return (s >= FIRST) & (s < nstep)

    def group_copy(t):
        return remote(sbuf.at[t], rbuf.at[g], ga_s, ga_r.at[g], {"group": t})

    def group_recv(s):
        return remote(sbuf.at[s], rbuf.at[s], ga_s, ga_r.at[s], {"group": s})

    sub = lax.broadcasted_iota(jnp.int32, (W, W), 0)
    lane = lax.broadcasted_iota(jnp.int32, (W, W), 1)
    nt = (((1,), (1,)), ((), ()))

    def give(i):
        t = (g + 1 + i) % ngroup

        @pl.when(t != g)
        def _():
            group_copy(t).start()

    def take(s, src):
        for c in range(2):
            place = (src[s, pl.ds(2 * W + 2 + c, 1), :] == sub.astype(F32)).astype(BF16)
            both = jnp.concatenate(split(src[s, pl.ds(c * W, W), :]), axis=0)
            got = lax.dot_general(both, place, nt, preferred_element_type=F32).astype(BF16)
            r = pl.ds(pl.multiple_of(s * 2 * W + c * W, W), W)
            hl[r, pl.ds(0, W)] = got[:W]
            hl[r, pl.ds(W, W)] = got[W:]

    def take_child(i):
        s = (g + ngroup - i) % ngroup

        @pl.when(i == 0)
        def _():
            take(g, sbuf)
            rbuf[g, pl.ds(2 * W, 8), :] = sbuf[g, pl.ds(2 * W, 8), :]

        @pl.when(i > 0)
        def _():
            group_recv(s).wait_recv()
            take(s, rbuf)

    PER = 16

    def extend(first):
        place = lax.broadcasted_iota(jnp.int32, (PAIR, W), 0).astype(F32)
        base = first.astype(F32)

        def body(q, acc):
            parts = []
            for i in range(PER):
                for c in range(2):
                    want = rbuf[q * PER + i, pl.ds(2 * W + c, 1), :] - base
                    parts.append(jnp.where(want == place, 1.0, 0.0).astype(BF16))
            hot = jnp.concatenate(parts, axis=1)
            r = pl.ds(pl.multiple_of(q * (PER * 2 * W), PER * 2 * W), PER * 2 * W)
            got = jnp.dot(hot, hl[r, :], preferred_element_type=F32)
            return acc + (got[:, :W] + got[:, W:])

        return lax.fori_loop(0, ngroup // PER, body, jnp.zeros((PAIR, W), F32))

    def product(prow, count):
        x = jnp.concatenate([pan[0, pl.ds(prow, count), :], pan[1, pl.ds(prow, count), :]], axis=1)
        hi, lo = split(x)
        got = jnp.dot(hi, xw[...], preferred_element_type=F32)
        return got[:, :W] + got[:, W:] + jnp.dot(lo, xw[:, :W], preferred_element_type=F32)

    def put(first, count, n):
        r = pl.ds(first, count)
        return pltpu.make_async_copy(mb.at[r], out.at[r], out_sem.at[n])

    def set_x(x):
        hi, lo = split(x)
        xw[:, pl.ds(0, W)] = hi
        xw[:, pl.ds(W, W)] = lo

    def pivot_rows():
        res = []
        for k in range(2):
            t = pan[k, pl.ds(256 * TSTEP + W * k, W), :]
            diag = jnp.sum(jnp.where(sub == lane, t, 0.0), axis=0, keepdims=True)
            res.append(1.0 / diag)
        return res

    def top_factor():
        d0, d1 = pivot_rows()
        piv[:, pl.ds(0, W)] = d0
        piv[:, pl.ds(W, W)] = d1

        @pl.when(z == 0)
        def _():
            set_x(-pan[yh, pl.ds(256 * TSTEP, 256), :])

        @pl.when(z != 0)
        def _():
            t = jnp.concatenate(
                [pan[0, pl.ds(256 * TSTEP, 256), :], pan[1, pl.ds(256 * TSTEP, 256), :]], axis=1
            )
            d = jnp.concatenate([d0, d1], axis=1)
            v = lax.dot_general(
                t, mb[pl.ds(0, 256), :], (((0,), (0,)), ((), ())),
                precision=HIGHEST, preferred_element_type=F32,
            )
            set_x(jnp.dot(t * d, v, precision=HIGHEST, preferred_element_type=F32))

    def top_output(e):
        keep = jnp.where(z == 0, 0.0, 1.0).astype(F32)
        r = pl.multiple_of(e * 256, 256)
        val = mb[pl.ds(r, 256), :] * keep - product(r, 256)
        row = lax.broadcasted_iota(jnp.int32, (256, W), 0) + r
        mb[pl.ds(r, 256), :] = jnp.where((row < W) & (b == 1), 0.0, val)
        put(r, 256, e).start()

    def late_output(u, extra):
        r = pl.multiple_of(TOP + PAIR * u, 128)
        mb[pl.ds(r, PAIR), :] = extra - product(pl.multiple_of(r + 256, 128), PAIR)
        put(r, PAIR, EARLY + u).start()

    def eliminate():
        x_ref[...] = (sub == lane).astype(F32)

        for lo in range(0, W, 32):
            rest = pl.ds(lo, W - lo)

            @pl.loop(lo, lo + 32)
            def _(j):
                s, x = s_ref[rest, :], x_ref[rest, :]
                srow, xrow = s_ref[pl.ds(j, 1), :], x_ref[pl.ds(j, 1), :]
                at = jnp.full((W - lo, W), j, jnp.int32)
                m = jnp.take_along_axis(s, at, axis=1)
                d = jnp.take_along_axis(jnp.broadcast_to(srow, (8, W)), at[:8], axis=1)[:1]
                m = jnp.where(sub[lo:] > j, m * (1.0 / d), 0.0)
                s_ref[rest, :] = s - m * srow
                x_ref[rest, :] = x - m * xrow

        d = jnp.sum(jnp.where(sub == lane, s_ref[...], 0.0), axis=0, keepdims=True)
        return jnp.transpose(x_ref[...]) * (1.0 / d)

    def factor():
        dot = functools.partial(jnp.dot, precision=HIGHEST, preferred_element_type=F32)
        base = 256 * TSTEP
        a01 = pan[1, pl.ds(0, W), :]
        s_ref[...] = pan[0, pl.ds(0, W), :]
        t00 = eliminate()
        pan[0, pl.ds(base, W), :] = t00
        pan[0, pl.ds(base + W, W), :] = jnp.zeros((W, W), F32)
        back01 = dot(t00, dot(x_ref[...], a01))
        s_ref[...] = pan[1, pl.ds(W, W), :] - lax.dot_general(
            a01, back01, (((0,), (0,)), ((), ())), precision=HIGHEST, preferred_element_type=F32
        )
        t11 = eliminate()
        pan[1, pl.ds(base + W, W), :] = t11
        pan[1, pl.ds(base, W), :] = -dot(back01, t11)

    @pl.when(z == 0)
    def _():
        get_top.wait()
        swap(0, 0, 256, yh).start()
        get_child.wait()

        @pl.loop(0, ngroup)
        def _(i):
            give(i)

            @pl.when(i == 3)
            def _():
                swap(0, 0, 256, other).wait_recv()
                big_z(0, 0, up).start()
                big_z(0, 1, down).start()

            @pl.when((i > 3) & (i < 3 + EARLY))
            def _():
                own_z(i - 3, 0, up, True).start()
                own_z(i - 3, 1, down, True).start()

        factor()
        big_z(TSTEP, 0, up).start()
        big_z(TSTEP, 1, down).start()
        get_front.wait()
        pl.loop(0, ngroup)(take_child)

        def own_send(s):
            swap(s, late_row(s), ZR, yh).start()
            own_z(s, 0, up, False).start()
            own_z(s, 1, down, False).start()

        def both_send(s):
            swap(s, late_row(s), ZR, other).wait_recv()
            late_z(s, 0, up).start()
            late_z(s, 1, down).start()

        @pl.loop(0, nlate // 2)
        def _(u):
            r = pl.multiple_of(TOP + PAIR * u, 128)
            val = mb[pl.ds(r, PAIR), :] + extend(r)
            pan[yh, pl.ds(pl.multiple_of(r + 256, 128), PAIR), :] = val
            s = FIRST + 2 * u
            own_send(s)
            own_send(s + 1)

            @pl.when(u > 0)
            def _():
                both_send(s - 2)
                both_send(s - 1)

        both_send(nstep - 2)
        both_send(nstep - 1)
        top_factor()
        top_output(0)

        @pl.loop(0, nlate // 2)
        def _(u):
            for i in range(2):
                for d in range(2):
                    back(FIRST + 2 * u + i, d, down, False).wait_recv()
            late_output(u, 0.0)

        @pl.loop(1, EARLY)
        def _(e):
            for d in range(2):
                back(e, d, down, True).wait_recv()
            top_output(e)

        swapped = pan.at[yh, pl.ds(0, 256 + nlate * ZR)]
        remote(swapped, swapped, yy_s.at[0], yy_r.at[0, 0], across).wait_send()
        for d in range(2):
            sent_z(d)

    @pl.when(z != 0)
    def _():
        lags = (HOP * (z - 1), HOP * (nz - 1 - z))
        devs = (up, down)
        last = (z < nz - 1, z > 1)
        turn = (z == 1, z == nz - 1)
        lag = HOP * (nz - 2) + CROSS
        get_child.wait()
        pl.loop(0, ngroup)(give)
        get_front.wait()

        def crossing(s):
            n = s - FIRST
            return jnp.where((n > 0) & (n % EVERY == 0) & (n < EVERY * EARLY), n // EVERY, 0)

        @pl.loop(0, nstep + lag)
        def _(t):
            for d in range(2):
                s = t - lags[d]

                @pl.when(is_big(s))
                def _(s=s, d=d):
                    big_z(s, d, devs[d]).wait_recv()

                    @pl.when(last[d])
                    def _():
                        big_z(s, d, devs[d]).start()

                for early, cond in ((True, is_early(s)), (False, is_late(s))):
                    @pl.when(cond)
                    def _(s=s, d=d, early=early):
                        own_z(s, d, devs[d], early).wait_recv()

                        @pl.when(last[d])
                        def _():
                            own_z(s, d, devs[d], early).start()

                        own_y(s, d, early).start()

            for d in range(2):
                s = t - lags[d] - CROSS
                e = crossing(s)

                @pl.when(is_late(s))
                def _(s=s, d=d):
                    late_z(s, d, devs[d]).wait_recv()

                    @pl.when(last[d])
                    def _():
                        late_z(s, d, devs[d]).start()

                for early, q, cond in ((False, s, is_late(s)), (True, e, e > 0)):
                    @pl.when(cond)
                    def _(q=q, d=d, early=early):
                        from_y(q, d, early).wait_recv()

                        @pl.when(turn[d])
                        def _():
                            back(q, d, devs[1 - d], early).start()

            s = t - lag
            n = s - FIRST

            @pl.when((n >= -8) & (n < 0))
            def _():
                take_child(2 * (n + 8))
                take_child(2 * (n + 8) + 1)

            @pl.when(s == TSTEP)
            def _():
                top_factor()
                top_output(0)

            @pl.when(crossing(s) > 0)
            def _():
                top_output(crossing(s))

            @pl.when((n > 0) & (n % 2 == 1))
            def _():
                u = n // 2
                r = pl.multiple_of(TOP + PAIR * u, 128)
                late_output(u, mb[pl.ds(r, PAIR), :] + extend(r))

        for d in range(2):
            own = pan.at[yh, pl.ds(0, own_rows)]
            remote(own, own, yy_s.at[d], yy_r.at[d, 0], across).wait_send()
            pl.when(last[d])(functools.partial(sent_z, d))

        @pl.when((z == 1) | (z == nz - 1))
        def _():
            own = pan.at[yh, pl.ds(0, own_rows)]
            remote(own, own, back_s, zy_r.at[0, 0], up).wait_send()

    given = sbuf.at[pl.ds(0, ngroup - 1)]
    remote(given, given, ga_s, ga_r.at[0], {"group": (g + 1) % ngroup}).wait_send()

    @pl.loop(0, EARLY)
    def _(e):
        put(pl.multiple_of(e * 256, 256), 256, e).wait()

    @pl.loop(0, nlate // 2)
    def _(u):
        put(pl.multiple_of(TOP + u * PAIR, 128), PAIR, EARLY + u).wait()


def per_device(ngroup, nblk, front, child_blocks, child_rows, child_cols, child_counts):
    rows = front.shape[1]
    slots = child_blocks.shape[3]
    nstep = FIRST + (rows - TOP) // STEP
    hbm = pl.BlockSpec(memory_space=pltpu.HBM)
    vmem = pl.BlockSpec(memory_space=pltpu.VMEM)
    smem = pl.BlockSpec(memory_space=pltpu.SMEM)
    dma = pltpu.SemaphoreType.DMA
    out, piv = pl.pallas_call(
        functools.partial(kernel, ngroup, nblk, rows),
        out_shape=(
            jax.ShapeDtypeStruct((rows, W), F32),
            jax.ShapeDtypeStruct((1, 2 * W), F32),
        ),
        in_specs=[hbm, hbm, vmem, vmem, smem],
        out_specs=(hbm, vmem),
        scratch_shapes=[
            pltpu.VMEM((rows, W), F32),
            pltpu.VMEM((2, rows + 256, W), F32),
            pltpu.VMEM((ngroup, slots * W + 8, W), F32),
            pltpu.VMEM((ngroup, slots * W + 8, W), F32),
            pltpu.VMEM((ngroup * slots * W, 2 * W), BF16),
            pltpu.VMEM((2 * W, 2 * W), BF16),
            pltpu.VMEM((W, W), F32),
            pltpu.VMEM((W, W), F32),
            dma((2,)), dma((2, nstep)), dma((2,)), dma((2, nstep)),
            dma((2,)), dma((2, nstep)), dma,
            dma, dma((ngroup,)),
            dma, dma, dma, dma((nstep,)),
        ],
        compiler_params=pltpu.CompilerParams(
            collective_id=0, has_side_effects=True, vmem_limit_bytes=56 * 2**20
        ),
        name="extend_and_factor",
    )(
        front[0], child_blocks.reshape(ngroup, slots * W, W), child_rows[0, 0],
        child_cols[0, 0], child_counts.reshape(1, ngroup),
    )
    return out[None], piv


def solution(mesh):
    in_specs = (
        P("group", None, "blk"),
        P("group", "blk", None, None, None, None),
        P("group", "blk", None, None, None),
        P("group", "blk", None, None, None),
        P("group", "blk", None),
    )
    out_specs = (P("group", None, "blk"), P("group", None))
    return jax.shard_map(
        functools.partial(per_device, mesh.shape["group"], mesh.shape["blk"]),
        mesh=mesh, in_specs=in_specs, out_specs=out_specs, check_vma=False,
    )
```

```python
import functools

import jax
import jax.numpy as jnp
from jax import lax
from jax.experimental import pallas as pl
from jax.experimental.pallas import tpu as pltpu
from jax.sharding import PartitionSpec as P

MESH = pl.DeviceIdType.MESH
F32 = jnp.float32
BF16 = jnp.bfloat16
HIGHEST = lax.Precision.HIGHEST

W = 128
TOP = 2048
EARLY = TOP // 256
TSTEP = EARLY
FIRST = TSTEP + 1
BASE = 256 * FIRST
ZR = 64
YR = 128
STEP = ZR + YR
PAIR = 2 * STEP
HOP = 3
CROSS = 4
AHEAD = 8
EVERY = 4


def split(x):
    hi = x.astype(BF16)
    return hi, (x - hi.astype(F32)).astype(BF16)


def remote(src, dst, send, recv, dev):
    return pltpu.make_async_remote_copy(
        src_ref=src, dst_ref=dst, send_sem=send, recv_sem=recv,
        device_id=dev, device_id_type=MESH,
    )


def kernel(
    ngroup, nblk, rows,
    front, child, child_rows, cols, counts,
    out, piv,
    mb, pan, sbuf, rbuf, hl, xw, s_ref, x_ref,
    zz_s, zz_r, zy_s, zy_r, yy_s, yy_r, back_s, ga_s, ga_r,
    in_sem, top_sem, child_sem, out_sem,
):
    g = lax.axis_index("group")
    b = lax.axis_index("blk")
    z, yh = b // 2, b % 2
    nz = nblk // 2
    other = 1 - yh
    up = {"blk": (b + 2) % nblk}
    down = {"blk": (b + nblk - 2) % nblk}
    across = {"blk": z * 2 + other}
    nlate = (rows - TOP) // STEP
    nstep = FIRST + nlate

    get_front = pltpu.make_async_copy(front, mb, in_sem)
    get_top = pltpu.make_async_copy(
        front.at[pl.ds(0, TOP)], pan.at[yh, pl.ds(0, TOP)], top_sem
    )
    get_child = pltpu.make_async_copy(child, sbuf.at[:, pl.ds(0, 2 * W)], child_sem)
    get_child.start()

    @pl.when(z == 0)
    def _():
        get_top.start()

    get_front.start()

    @pl.loop(0, ngroup)
    def _(t):
        slot = lax.broadcasted_iota(jnp.int32, (2, W), 0)
        at = jnp.where(slot < counts[0, t], child_rows[t], -1)
        sbuf[t, pl.ds(2 * W, 2), :] = at.astype(F32)
        sbuf[t, pl.ds(2 * W + 2, 2), :] = cols[t].astype(F32)

    barrier = pltpu.get_barrier_semaphore()
    for i in range(1, ngroup):
        pl.semaphore_signal(
            barrier, inc=1, device_id={"group": (g + i) % ngroup}, device_id_type=MESH
        )
    for dev in (up, down, across):
        pl.semaphore_signal(barrier, inc=1, device_id=dev, device_id_type=MESH)
    pl.semaphore_wait(barrier, ngroup - 1 + 3)

    def late_row(s):
        return BASE + STEP * (s - FIRST)

    def big_z(s, d, dev):
        r = pl.ds(pl.multiple_of(256 * s + 128 * d, 128), 128)
        return remote(pan.at[:, r], pan.at[:, r], zz_s.at[d], zz_r.at[d, s], dev)

    def late_z(s, d, dev):
        r = pl.ds(pl.multiple_of(late_row(s) + ZR // 2 * d, ZR // 2), ZR // 2)
        return remote(pan.at[:, r], pan.at[:, r], zz_s.at[d], zz_r.at[d, s], dev)

    def y_rows(s, d, early):
        if early:
            return pl.ds(pl.multiple_of(256 * s + 128 * d, 128), 128)
        half = YR // 2
        return pl.ds(pl.multiple_of(late_row(s) + ZR + half * d, half), half)

    def own_z(s, d, dev, early):
        r = y_rows(s, d, early)
        return remote(pan.at[yh, r], pan.at[yh, r], zy_s.at[d], zy_r.at[d, s], dev)

    def own_y(s, d, early):
        r = y_rows(s, d, early)
        return remote(pan.at[yh, r], pan.at[yh, r], yy_s.at[d], yy_r.at[d, s], across)

    def from_y(s, d, early):
        r = y_rows(s, d, early)
        return remote(pan.at[other, r], pan.at[other, r], yy_s.at[d], yy_r.at[d, s], across)

    def back(s, d, dev, early):
        r = y_rows(s, d, early)
        return remote(pan.at[other, r], pan.at[other, r], back_s, zy_r.at[d, s], dev)

    def swap(s, start, count, k):
        r = pl.ds(pl.multiple_of(start, count), count)
        return remote(pan.at[k, r], pan.at[k, r], yy_s.at[0], yy_r.at[0, s], across)

    own_rows = (EARLY - 1) * W + nlate * (YR // 2)

    def sent_z(d):
        dev = (up, down)[d]
        own = pan.at[yh, pl.ds(0, own_rows)]
        remote(own, own, zy_s.at[d], zy_r.at[d, 0], dev).wait_send()
        both = pan.at[:, pl.ds(0, 2 * W + nlate * (ZR // 2))]
        remote(both, both, zz_s.at[d], zz_r.at[d, 0], dev).wait_send()

    def is_big(s):
        return (s == 0) | (s == TSTEP)

    def is_early(s):
        return (s >= 1) & (s < TSTEP)

    def is_late(s):
        return (s >= FIRST) & (s < nstep)

    def group_copy(t):
        return remote(sbuf.at[t], rbuf.at[g], ga_s, ga_r.at[g], {"group": t})

    def group_recv(s):
        return remote(sbuf.at[s], rbuf.at[s], ga_s, ga_r.at[s], {"group": s})

    sub = lax.broadcasted_iota(jnp.int32, (W, W), 0)
    lane = lax.broadcasted_iota(jnp.int32, (W, W), 1)
    nt = (((1,), (1,)), ((), ()))

    def give(i):
        t = (g + 1 + i) % ngroup

        @pl.when(t != g)
        def _():
            group_copy(t).start()

    def take(s, src):
        for c in range(2):
            place = (src[s, pl.ds(2 * W + 2 + c, 1), :] == sub.astype(F32)).astype(BF16)
            both = jnp.concatenate(split(src[s, pl.ds(c * W, W), :]), axis=0)
            got = lax.dot_general(both, place, nt, preferred_element_type=F32).astype(BF16)
            r = pl.ds(pl.multiple_of(s * 2 * W + c * W, W), W)
            hl[r, pl.ds(0, W)] = got[:W]
            hl[r, pl.ds(W, W)] = got[W:]

    def take_child(i):
        s = (g + ngroup - i) % ngroup

        @pl.when(i == 0)
        def _():
            take(g, sbuf)
            rbuf[g, pl.ds(2 * W, 8), :] = sbuf[g, pl.ds(2 * W, 8), :]

        @pl.when(i > 0)
        def _():
            group_recv(s).wait_recv()
            take(s, rbuf)

    def extend(first, lo, count):
        place = lax.broadcasted_iota(jnp.int32, (PAIR, W), 0).astype(F32)
        base = first.astype(F32)
        parts = []
        for i in range(lo, lo + count):
            for c in range(2):
                want = rbuf[i, pl.ds(2 * W + c, 1), :] - base
                parts.append(jnp.where(want == place, 1.0, 0.0).astype(BF16))
        hot = jnp.concatenate(parts, axis=1)
        got = jnp.dot(
            hot, hl[pl.ds(lo * 2 * W, count * 2 * W), :], preferred_element_type=F32
        )
        return got[:, :W] + got[:, W:]

    def product(prow, count):
        x = jnp.concatenate([pan[0, pl.ds(prow, count), :], pan[1, pl.ds(prow, count), :]], axis=1)
        hi, lo = split(x)
        got = jnp.dot(hi, xw[...], preferred_element_type=F32)
        return got[:, :W] + got[:, W:] + jnp.dot(lo, xw[:, :W], preferred_element_type=F32)

    def put(first, count, n):
        r = pl.ds(first, count)
        return pltpu.make_async_copy(mb.at[r], out.at[r], out_sem.at[n])

    def set_x(x):
        hi, lo = split(x)
        xw[:, pl.ds(0, W)] = hi
        xw[:, pl.ds(W, W)] = lo

    def pivot_rows():
        res = []
        for k in range(2):
            t = pan[k, pl.ds(256 * TSTEP + W * k, W), :]
            diag = jnp.sum(jnp.where(sub == lane, t, 0.0), axis=0, keepdims=True)
            res.append(1.0 / diag)
        return res

    def top_factor():
        d0, d1 = pivot_rows()
        piv[:, pl.ds(0, W)] = d0
        piv[:, pl.ds(W, W)] = d1

        @pl.when(z == 0)
        def _():
            set_x(-pan[yh, pl.ds(256 * TSTEP, 256), :])

        @pl.when(z != 0)
        def _():
            t = jnp.concatenate(
                [pan[0, pl.ds(256 * TSTEP, 256), :], pan[1, pl.ds(256 * TSTEP, 256), :]], axis=1
            )
            d = jnp.concatenate([d0, d1], axis=1)
            v = lax.dot_general(
                t, mb[pl.ds(0, 256), :], (((0,), (0,)), ((), ())),
                precision=HIGHEST, preferred_element_type=F32,
            )
            set_x(jnp.dot(t * d, v, precision=HIGHEST, preferred_element_type=F32))

    def top_output(e):
        keep = jnp.where(z == 0, 0.0, 1.0).astype(F32)
        r = pl.multiple_of(e * 256, 256)
        val = mb[pl.ds(r, 256), :] * keep - product(r, 256)
        row = lax.broadcasted_iota(jnp.int32, (256, W), 0) + r
        mb[pl.ds(r, 256), :] = jnp.where((row < W) & (b == 1), 0.0, val)
        put(r, 256, e).start()

    def late_output(u, extra):
        r = pl.multiple_of(TOP + PAIR * u, 128)
        mb[pl.ds(r, PAIR), :] = extra - product(pl.multiple_of(r + 256, 128), PAIR)
        put(r, PAIR, EARLY + u).start()

    def eliminate():
        x_ref[...] = (sub == lane).astype(F32)

        for lo in range(0, W, 32):
            rest = pl.ds(lo, W - lo)

            @pl.loop(lo, lo + 32)
            def _(j):
                s, x = s_ref[rest, :], x_ref[rest, :]
                srow, xrow = s_ref[pl.ds(j, 1), :], x_ref[pl.ds(j, 1), :]
                at = jnp.full((W - lo, W), j, jnp.int32)
                m = jnp.take_along_axis(s, at, axis=1)
                d = jnp.take_along_axis(jnp.broadcast_to(srow, (8, W)), at[:8], axis=1)[:1]
                m = jnp.where(sub[lo:] > j, m * (1.0 / d), 0.0)
                s_ref[rest, :] = s - m * srow
                x_ref[rest, :] = x - m * xrow

        d = jnp.sum(jnp.where(sub == lane, s_ref[...], 0.0), axis=0, keepdims=True)
        return jnp.transpose(x_ref[...]) * (1.0 / d)

    def factor():
        dot = functools.partial(jnp.dot, precision=HIGHEST, preferred_element_type=F32)
        base = 256 * TSTEP
        a01 = pan[1, pl.ds(0, W), :]
        s_ref[...] = pan[0, pl.ds(0, W), :]
        t00 = eliminate()
        pan[0, pl.ds(base, W), :] = t00
        pan[0, pl.ds(base + W, W), :] = jnp.zeros((W, W), F32)
        back01 = dot(t00, dot(x_ref[...], a01))
        s_ref[...] = pan[1, pl.ds(W, W), :] - lax.dot_general(
            a01, back01, (((0,), (0,)), ((), ())), precision=HIGHEST, preferred_element_type=F32
        )
        t11 = eliminate()
        pan[1, pl.ds(base + W, W), :] = t11
        pan[1, pl.ds(base, W), :] = -dot(back01, t11)

    @pl.when(z == 0)
    def _():
        get_top.wait()
        swap(0, 0, 256, yh).start()
        get_child.wait()

        @pl.loop(0, ngroup)
        def _(i):
            give(i)

            @pl.when(i == 3)
            def _():
                swap(0, 0, 256, other).wait_recv()
                big_z(0, 0, up).start()
                big_z(0, 1, down).start()

            @pl.when((i > 3) & (i < 3 + EARLY))
            def _():
                own_z(i - 3, 0, up, True).start()
                own_z(i - 3, 1, down, True).start()

        factor()
        big_z(TSTEP, 0, up).start()
        big_z(TSTEP, 1, down).start()
        get_front.wait()
        pl.loop(0, ngroup)(take_child)

        def own_send(s):
            swap(s, late_row(s), ZR, yh).start()
            own_z(s, 0, up, False).start()
            own_z(s, 1, down, False).start()

        def both_send(s):
            swap(s, late_row(s), ZR, other).wait_recv()
            late_z(s, 0, up).start()
            late_z(s, 1, down).start()

        @pl.loop(0, nlate // 2)
        def _(u):
            r = pl.multiple_of(TOP + PAIR * u, 128)
            val = mb[pl.ds(r, PAIR), :] + extend(r, 0, ngroup)
            pan[yh, pl.ds(pl.multiple_of(r + 256, 128), PAIR), :] = val
            s = FIRST + 2 * u
            own_send(s)
            own_send(s + 1)

            @pl.when(u > 0)
            def _():
                both_send(s - 2)
                both_send(s - 1)

        both_send(nstep - 2)
        both_send(nstep - 1)
        top_factor()
        top_output(0)

        @pl.loop(0, nlate // 2)
        def _(u):
            for i in range(2):
                for d in range(2):
                    back(FIRST + 2 * u + i, d, down, False).wait_recv()
            late_output(u, 0.0)

        @pl.loop(1, EARLY)
        def _(e):
            for d in range(2):
                back(e, d, down, True).wait_recv()
            top_output(e)

        swapped = pan.at[yh, pl.ds(0, 256 + nlate * ZR)]
        remote(swapped, swapped, yy_s.at[0], yy_r.at[0, 0], across).wait_send()
        for d in range(2):
            sent_z(d)

    @pl.when(z != 0)
    def _():
        lags = (HOP * (z - 1), HOP * (nz - 1 - z))
        devs = (up, down)
        last = (z < nz - 1, z > 1)
        turn = (z == 1, z == nz - 1)
        lag = HOP * (nz - 2) + CROSS
        get_child.wait()
        pl.loop(0, ngroup)(give)
        get_front.wait()

        def crossing(s):
            n = s - FIRST
            return jnp.where((n > 0) & (n % EVERY == 0) & (n < EVERY * EARLY), n // EVERY, 0)

        @pl.loop(0, nstep + lag)
        def _(t):
            for d in range(2):
                s = t - lags[d]

                @pl.when(is_big(s))
                def _(s=s, d=d):
                    big_z(s, d, devs[d]).wait_recv()

                    @pl.when(last[d])
                    def _():
                        big_z(s, d, devs[d]).start()

                for early, cond in ((True, is_early(s)), (False, is_late(s))):
                    @pl.when(cond)
                    def _(s=s, d=d, early=early):
                        own_z(s, d, devs[d], early).wait_recv()

                        @pl.when(last[d])
                        def _():
                            own_z(s, d, devs[d], early).start()

                        own_y(s, d, early).start()

            for d in range(2):
                s = t - lags[d] - CROSS
                e = crossing(s)

                @pl.when(is_late(s))
                def _(s=s, d=d):
                    late_z(s, d, devs[d]).wait_recv()

                    @pl.when(last[d])
                    def _():
                        late_z(s, d, devs[d]).start()

                for early, q, cond in ((False, s, is_late(s)), (True, e, e > 0)):
                    @pl.when(cond)
                    def _(q=q, d=d, early=early):
                        from_y(q, d, early).wait_recv()

                        @pl.when(turn[d])
                        def _():
                            back(q, d, devs[1 - d], early).start()

            s = t - lag
            n = s - FIRST

            m = n + AHEAD

            @pl.when((m >= -8) & (m < 0))
            def _():
                take_child(2 * (m + 8))
                take_child(2 * (m + 8) + 1)

            @pl.when(s == TSTEP)
            def _():
                top_factor()
                top_output(0)

            @pl.when(crossing(s) > 0)
            def _():
                top_output(crossing(s))

            half = ngroup // 2

            @pl.when((m >= 0) & (m < nlate))
            def _():
                r = pl.multiple_of(TOP + PAIR * (m // 2), 128)

                @pl.when(m % 2 == 0)
                def _():
                    mb[pl.ds(r, PAIR), :] += extend(r, 0, half)

                @pl.when(m % 2 == 1)
                def _():
                    mb[pl.ds(r, PAIR), :] += extend(r, half, half)

            @pl.when((n > 0) & (n % 2 == 1))
            def _():
                u = n // 2
                late_output(u, mb[pl.ds(pl.multiple_of(TOP + PAIR * u, 128), PAIR), :])

        for d in range(2):
            own = pan.at[yh, pl.ds(0, own_rows)]
            remote(own, own, yy_s.at[d], yy_r.at[d, 0], across).wait_send()
            pl.when(last[d])(functools.partial(sent_z, d))

        @pl.when((z == 1) | (z == nz - 1))
        def _():
            own = pan.at[yh, pl.ds(0, own_rows)]
            remote(own, own, back_s, zy_r.at[0, 0], up).wait_send()

    given = sbuf.at[pl.ds(0, ngroup - 1)]
    remote(given, given, ga_s, ga_r.at[0], {"group": (g + 1) % ngroup}).wait_send()

    @pl.loop(0, EARLY)
    def _(e):
        put(pl.multiple_of(e * 256, 256), 256, e).wait()

    @pl.loop(0, nlate // 2)
    def _(u):
        put(pl.multiple_of(TOP + u * PAIR, 128), PAIR, EARLY + u).wait()


def per_device(ngroup, nblk, front, child_blocks, child_rows, child_cols, child_counts):
    rows = front.shape[1]
    slots = child_blocks.shape[3]
    nstep = FIRST + (rows - TOP) // STEP
    hbm = pl.BlockSpec(memory_space=pltpu.HBM)
    vmem = pl.BlockSpec(memory_space=pltpu.VMEM)
    smem = pl.BlockSpec(memory_space=pltpu.SMEM)
    dma = pltpu.SemaphoreType.DMA
    out, piv = pl.pallas_call(
        functools.partial(kernel, ngroup, nblk, rows),
        out_shape=(
            jax.ShapeDtypeStruct((rows, W), F32),
            jax.ShapeDtypeStruct((1, 2 * W), F32),
        ),
        in_specs=[hbm, hbm, vmem, vmem, smem],
        out_specs=(hbm, vmem),
        scratch_shapes=[
            pltpu.VMEM((rows, W), F32),
            pltpu.VMEM((2, rows + 256, W), F32),
            pltpu.VMEM((ngroup, slots * W + 8, W), F32),
            pltpu.VMEM((ngroup, slots * W + 8, W), F32),
            pltpu.VMEM((ngroup * slots * W, 2 * W), BF16),
            pltpu.VMEM((2 * W, 2 * W), BF16),
            pltpu.VMEM((W, W), F32),
            pltpu.VMEM((W, W), F32),
            dma((2,)), dma((2, nstep)), dma((2,)), dma((2, nstep)),
            dma((2,)), dma((2, nstep)), dma,
            dma, dma((ngroup,)),
            dma, dma, dma, dma((nstep,)),
        ],
        compiler_params=pltpu.CompilerParams(
            collective_id=0, has_side_effects=True, vmem_limit_bytes=56 * 2**20
        ),
        name="extend_and_factor",
    )(
        front[0], child_blocks.reshape(ngroup, slots * W, W), child_rows[0, 0],
        child_cols[0, 0], child_counts.reshape(1, ngroup),
    )
    return out[None], piv


def solution(mesh):
    in_specs = (
        P("group", None, "blk"),
        P("group", "blk", None, None, None, None),
        P("group", "blk", None, None, None),
        P("group", "blk", None, None, None),
        P("group", "blk", None),
    )
    out_specs = (P("group", None, "blk"), P("group", None))
    return jax.shard_map(
        functools.partial(per_device, mesh.shape["group"], mesh.shape["blk"]),
        mesh=mesh, in_specs=in_specs, out_specs=out_specs, check_vma=False,
    )
```

```python
import functools

import jax
import jax.numpy as jnp
from jax import lax
from jax.experimental import pallas as pl
from jax.experimental.pallas import tpu as pltpu
from jax.sharding import PartitionSpec as P

MESH = pl.DeviceIdType.MESH
F32 = jnp.float32
BF16 = jnp.bfloat16
HIGHEST = lax.Precision.HIGHEST

W = 128
TOP = 2048
EARLY = TOP // 256
TSTEP = EARLY
FIRST = TSTEP + 1
BASE = 256 * FIRST
ZR = 64
YR = 128
STEP = ZR + YR
PAIR = 2 * STEP
HOP = 3
CROSS = 4
AHEAD = 8
EVERY = 4


def split(x):
    hi = x.astype(BF16)
    return hi, (x - hi.astype(F32)).astype(BF16)


def remote(src, dst, send, recv, dev):
    return pltpu.make_async_remote_copy(
        src_ref=src, dst_ref=dst, send_sem=send, recv_sem=recv,
        device_id=dev, device_id_type=MESH,
    )


def kernel(
    ngroup, nblk, rows,
    front, child, child_rows, cols, counts,
    out, piv,
    mb, pan, sbuf, rbuf, hl, xw, s_ref, x_ref,
    zz_s, zz_r, zy_s, zy_r, yy_s, yy_r, back_s, ga_s, ga_r,
    in_sem, top_sem, child_sem, out_sem,
):
    g = lax.axis_index("group")
    b = lax.axis_index("blk")
    z, yh = b // 2, b % 2
    nz = nblk // 2
    other = 1 - yh
    up = {"blk": (b + 2) % nblk}
    down = {"blk": (b + nblk - 2) % nblk}
    across = {"blk": z * 2 + other}
    nlate = (rows - TOP) // STEP
    nstep = FIRST + nlate

    get_front = pltpu.make_async_copy(front, mb, in_sem)
    get_top = pltpu.make_async_copy(
        front.at[pl.ds(0, TOP)], pan.at[yh, pl.ds(0, TOP)], top_sem
    )
    get_child = pltpu.make_async_copy(child, sbuf.at[:, pl.ds(0, 2 * W)], child_sem)
    get_child.start()

    @pl.when(z == 0)
    def _():
        get_top.start()

    get_front.start()

    @pl.loop(0, ngroup)
    def _(t):
        slot = lax.broadcasted_iota(jnp.int32, (2, W), 0)
        at = jnp.where(slot < counts[0, t], child_rows[t], -1)
        sbuf[t, pl.ds(2 * W, 2), :] = at.astype(F32)
        sbuf[t, pl.ds(2 * W + 2, 2), :] = cols[t].astype(F32)

    barrier = pltpu.get_barrier_semaphore()
    for i in range(1, ngroup):
        pl.semaphore_signal(
            barrier, inc=1, device_id={"group": (g + i) % ngroup}, device_id_type=MESH
        )
    for dev in (up, down, across):
        pl.semaphore_signal(barrier, inc=1, device_id=dev, device_id_type=MESH)
    pl.semaphore_wait(barrier, ngroup - 1 + 3)

    def late_row(s):
        return BASE + STEP * (s - FIRST)

    def big_z(s, d, dev):
        r = pl.ds(pl.multiple_of(256 * s + 128 * d, 128), 128)
        return remote(pan.at[:, r], pan.at[:, r], zz_s.at[d], zz_r.at[d, s], dev)

    def late_z(s, d, dev):
        r = pl.ds(pl.multiple_of(late_row(s) + ZR // 2 * d, ZR // 2), ZR // 2)
        return remote(pan.at[:, r], pan.at[:, r], zz_s.at[d], zz_r.at[d, s], dev)

    def y_rows(s, d, early):
        if early:
            return pl.ds(pl.multiple_of(256 * s + 128 * d, 128), 128)
        half = YR // 2
        return pl.ds(pl.multiple_of(late_row(s) + ZR + half * d, half), half)

    def own_z(s, d, dev, early):
        r = y_rows(s, d, early)
        return remote(pan.at[yh, r], pan.at[yh, r], zy_s.at[d], zy_r.at[d, s], dev)

    def own_y(s, d, early):
        r = y_rows(s, d, early)
        return remote(pan.at[yh, r], pan.at[yh, r], yy_s.at[d], yy_r.at[d, s], across)

    def from_y(s, d, early):
        r = y_rows(s, d, early)
        return remote(pan.at[other, r], pan.at[other, r], yy_s.at[d], yy_r.at[d, s], across)

    def back(s, d, dev, early):
        r = y_rows(s, d, early)
        return remote(pan.at[other, r], pan.at[other, r], back_s, zy_r.at[d, s], dev)

    def swap(s, start, count, k):
        r = pl.ds(pl.multiple_of(start, count), count)
        return remote(pan.at[k, r], pan.at[k, r], yy_s.at[0], yy_r.at[0, s], across)

    own_rows = (EARLY - 1) * W + nlate * (YR // 2)

    def sent_z(d):
        dev = (up, down)[d]
        own = pan.at[yh, pl.ds(0, own_rows)]
        remote(own, own, zy_s.at[d], zy_r.at[d, 0], dev).wait_send()
        both = pan.at[:, pl.ds(0, 2 * W + nlate * (ZR // 2))]
        remote(both, both, zz_s.at[d], zz_r.at[d, 0], dev).wait_send()

    def is_big(s):
        return (s == 0) | (s == TSTEP)

    def is_early(s):
        return (s >= 1) & (s < TSTEP)

    def is_late(s):
        return (s >= FIRST) & (s < nstep)

    def group_copy(t):
        return remote(sbuf.at[t], rbuf.at[g], ga_s, ga_r.at[g], {"group": t})

    def group_recv(s):
        return remote(sbuf.at[s], rbuf.at[s], ga_s, ga_r.at[s], {"group": s})

    sub = lax.broadcasted_iota(jnp.int32, (W, W), 0)
    lane = lax.broadcasted_iota(jnp.int32, (W, W), 1)
    nt = (((1,), (1,)), ((), ()))

    def partner(i, sign):
        n = (7 * i) % ngroup
        core = (g + n) % 2
        y = (g // 2 + n // 2) % 2
        x = (g // 4 + sign * (n // 4) + ngroup // 4) % (ngroup // 4)
        return x * 4 + y * 2 + core

    def give(i):
        group_copy(partner(i, 1)).start()

    def take(s, src):
        for c in range(2):
            place = (src[s, pl.ds(2 * W + 2 + c, 1), :] == sub.astype(F32)).astype(BF16)
            both = jnp.concatenate(split(src[s, pl.ds(c * W, W), :]), axis=0)
            got = lax.dot_general(both, place, nt, preferred_element_type=F32).astype(BF16)
            r = pl.ds(pl.multiple_of(s * 2 * W + c * W, W), W)
            hl[r, pl.ds(0, W)] = got[:W]
            hl[r, pl.ds(W, W)] = got[W:]

    def take_child(i):
        s = partner(i, -1)

        @pl.when(i == 0)
        def _():
            take(g, sbuf)
            rbuf[g, pl.ds(2 * W, 8), :] = sbuf[g, pl.ds(2 * W, 8), :]

        @pl.when(i > 0)
        def _():
            group_recv(s).wait_recv()
            take(s, rbuf)

    def extend(first, lo, count):
        place = lax.broadcasted_iota(jnp.int32, (PAIR, W), 0).astype(F32)
        base = first.astype(F32)
        parts = []
        for i in range(lo, lo + count):
            for c in range(2):
                want = rbuf[i, pl.ds(2 * W + c, 1), :] - base
                parts.append(jnp.where(want == place, 1.0, 0.0).astype(BF16))
        hot = jnp.concatenate(parts, axis=1)
        got = jnp.dot(
            hot, hl[pl.ds(lo * 2 * W, count * 2 * W), :], preferred_element_type=F32
        )
        return got[:, :W] + got[:, W:]

    def product(prow, count):
        x = jnp.concatenate([pan[0, pl.ds(prow, count), :], pan[1, pl.ds(prow, count), :]], axis=1)
        hi, lo = split(x)
        got = jnp.dot(hi, xw[...], preferred_element_type=F32)
        return got[:, :W] + got[:, W:] + jnp.dot(lo, xw[:, :W], preferred_element_type=F32)

    def put(first, count, n):
        r = pl.ds(first, count)
        return pltpu.make_async_copy(mb.at[r], out.at[r], out_sem.at[n])

    def set_x(x):
        hi, lo = split(x)
        xw[:, pl.ds(0, W)] = hi
        xw[:, pl.ds(W, W)] = lo

    def pivot_rows():
        res = []
        for k in range(2):
            t = pan[k, pl.ds(256 * TSTEP + W * k, W), :]
            diag = jnp.sum(jnp.where(sub == lane, t, 0.0), axis=0, keepdims=True)
            res.append(1.0 / diag)
        return res

    def top_factor():
        d0, d1 = pivot_rows()
        piv[:, pl.ds(0, W)] = d0
        piv[:, pl.ds(W, W)] = d1

        @pl.when(z == 0)
        def _():
            set_x(-pan[yh, pl.ds(256 * TSTEP, 256), :])

        @pl.when(z != 0)
        def _():
            t = jnp.concatenate(
                [pan[0, pl.ds(256 * TSTEP, 256), :], pan[1, pl.ds(256 * TSTEP, 256), :]], axis=1
            )
            d = jnp.concatenate([d0, d1], axis=1)
            v = lax.dot_general(
                t, mb[pl.ds(0, 256), :], (((0,), (0,)), ((), ())),
                precision=HIGHEST, preferred_element_type=F32,
            )
            set_x(jnp.dot(t * d, v, precision=HIGHEST, preferred_element_type=F32))

    def top_output(e):
        keep = jnp.where(z == 0, 0.0, 1.0).astype(F32)
        r = pl.multiple_of(e * 256, 256)
        val = mb[pl.ds(r, 256), :] * keep - product(r, 256)
        row = lax.broadcasted_iota(jnp.int32, (256, W), 0) + r
        mb[pl.ds(r, 256), :] = jnp.where((row < W) & (b == 1), 0.0, val)
        put(r, 256, e).start()

    def late_output(u, extra):
        r = pl.multiple_of(TOP + PAIR * u, 128)
        mb[pl.ds(r, PAIR), :] = extra - product(pl.multiple_of(r + 256, 128), PAIR)
        put(r, PAIR, EARLY + u).start()

    def eliminate():
        x_ref[...] = (sub == lane).astype(F32)

        for lo in range(0, W, 32):
            rest = pl.ds(lo, W - lo)

            @pl.loop(lo, lo + 32)
            def _(j):
                s, x = s_ref[rest, :], x_ref[rest, :]
                srow, xrow = s_ref[pl.ds(j, 1), :], x_ref[pl.ds(j, 1), :]
                at = jnp.full((W - lo, W), j, jnp.int32)
                m = jnp.take_along_axis(s, at, axis=1)
                d = jnp.take_along_axis(jnp.broadcast_to(srow, (8, W)), at[:8], axis=1)[:1]
                m = jnp.where(sub[lo:] > j, m * (1.0 / d), 0.0)
                s_ref[rest, :] = s - m * srow
                x_ref[rest, :] = x - m * xrow

        d = jnp.sum(jnp.where(sub == lane, s_ref[...], 0.0), axis=0, keepdims=True)
        return jnp.transpose(x_ref[...]) * (1.0 / d)

    def factor():
        dot = functools.partial(jnp.dot, precision=HIGHEST, preferred_element_type=F32)
        base = 256 * TSTEP
        a01 = pan[1, pl.ds(0, W), :]
        s_ref[...] = pan[0, pl.ds(0, W), :]
        t00 = eliminate()
        pan[0, pl.ds(base, W), :] = t00
        pan[0, pl.ds(base + W, W), :] = jnp.zeros((W, W), F32)
        back01 = dot(t00, dot(x_ref[...], a01))
        s_ref[...] = pan[1, pl.ds(W, W), :] - lax.dot_general(
            a01, back01, (((0,), (0,)), ((), ())), precision=HIGHEST, preferred_element_type=F32
        )
        t11 = eliminate()
        pan[1, pl.ds(base + W, W), :] = t11
        pan[1, pl.ds(base, W), :] = -dot(back01, t11)

    @pl.when(z == 0)
    def _():
        get_top.wait()
        swap(0, 0, 256, yh).start()
        get_child.wait()

        @pl.loop(0, ngroup)
        def _(i):
            pl.when(i > 0)(functools.partial(give, i))

            @pl.when(i == 3)
            def _():
                swap(0, 0, 256, other).wait_recv()
                big_z(0, 0, up).start()
                big_z(0, 1, down).start()

            @pl.when((i > 3) & (i < 3 + EARLY))
            def _():
                own_z(i - 3, 0, up, True).start()
                own_z(i - 3, 1, down, True).start()

        factor()
        big_z(TSTEP, 0, up).start()
        big_z(TSTEP, 1, down).start()
        get_front.wait()
        pl.loop(0, ngroup)(take_child)

        def own_send(s):
            swap(s, late_row(s), ZR, yh).start()
            own_z(s, 0, up, False).start()
            own_z(s, 1, down, False).start()

        def both_send(s):
            swap(s, late_row(s), ZR, other).wait_recv()
            late_z(s, 0, up).start()
            late_z(s, 1, down).start()

        @pl.loop(0, nlate // 2)
        def _(u):
            r = pl.multiple_of(TOP + PAIR * u, 128)
            val = mb[pl.ds(r, PAIR), :] + extend(r, 0, ngroup)
            pan[yh, pl.ds(pl.multiple_of(r + 256, 128), PAIR), :] = val
            s = FIRST + 2 * u
            own_send(s)
            own_send(s + 1)

            @pl.when(u > 0)
            def _():
                both_send(s - 2)
                both_send(s - 1)

        both_send(nstep - 2)
        both_send(nstep - 1)
        top_factor()
        top_output(0)

        @pl.loop(0, nlate // 2)
        def _(u):
            for i in range(2):
                for d in range(2):
                    back(FIRST + 2 * u + i, d, down, False).wait_recv()
            late_output(u, 0.0)

        @pl.loop(1, EARLY)
        def _(e):
            for d in range(2):
                back(e, d, down, True).wait_recv()
            top_output(e)

        swapped = pan.at[yh, pl.ds(0, 256 + nlate * ZR)]
        remote(swapped, swapped, yy_s.at[0], yy_r.at[0, 0], across).wait_send()
        for d in range(2):
            sent_z(d)

    @pl.when(z != 0)
    def _():
        lags = (HOP * (z - 1), HOP * (nz - 1 - z))
        devs = (up, down)
        last = (z < nz - 1, z > 1)
        turn = (z == 1, z == nz - 1)
        lag = HOP * (nz - 2) + CROSS
        get_child.wait()
        pl.loop(1, ngroup)(give)
        get_front.wait()

        def crossing(s):
            n = s - FIRST
            return jnp.where((n > 0) & (n % EVERY == 0) & (n < EVERY * EARLY), n // EVERY, 0)

        @pl.loop(0, nstep + lag)
        def _(t):
            for d in range(2):
                s = t - lags[d]

                @pl.when(is_big(s))
                def _(s=s, d=d):
                    big_z(s, d, devs[d]).wait_recv()

                    @pl.when(last[d])
                    def _():
                        big_z(s, d, devs[d]).start()

                for early, cond in ((True, is_early(s)), (False, is_late(s))):
                    @pl.when(cond)
                    def _(s=s, d=d, early=early):
                        own_z(s, d, devs[d], early).wait_recv()

                        @pl.when(last[d])
                        def _():
                            own_z(s, d, devs[d], early).start()

                        own_y(s, d, early).start()

            for d in range(2):
                s = t - lags[d] - CROSS
                e = crossing(s)

                @pl.when(is_late(s))
                def _(s=s, d=d):
                    late_z(s, d, devs[d]).wait_recv()

                    @pl.when(last[d])
                    def _():
                        late_z(s, d, devs[d]).start()

                for early, q, cond in ((False, s, is_late(s)), (True, e, e > 0)):
                    @pl.when(cond)
                    def _(q=q, d=d, early=early):
                        from_y(q, d, early).wait_recv()

                        @pl.when(turn[d])
                        def _():
                            back(q, d, devs[1 - d], early).start()

            s = t - lag
            n = s - FIRST

            m = n + AHEAD

            @pl.when((m >= -8) & (m < 0))
            def _():
                take_child(2 * (m + 8))
                take_child(2 * (m + 8) + 1)

            @pl.when(s == TSTEP)
            def _():
                top_factor()
                top_output(0)

            @pl.when(crossing(s) > 0)
            def _():
                top_output(crossing(s))

            half = ngroup // 2

            @pl.when((m >= 0) & (m < nlate))
            def _():
                r = pl.multiple_of(TOP + PAIR * (m // 2), 128)

                @pl.when(m % 2 == 0)
                def _():
                    mb[pl.ds(r, PAIR), :] += extend(r, 0, half)

                @pl.when(m % 2 == 1)
                def _():
                    mb[pl.ds(r, PAIR), :] += extend(r, half, half)

            @pl.when((n > 0) & (n % 2 == 1))
            def _():
                u = n // 2
                late_output(u, mb[pl.ds(pl.multiple_of(TOP + PAIR * u, 128), PAIR), :])

        for d in range(2):
            own = pan.at[yh, pl.ds(0, own_rows)]
            remote(own, own, yy_s.at[d], yy_r.at[d, 0], across).wait_send()
            pl.when(last[d])(functools.partial(sent_z, d))

        @pl.when((z == 1) | (z == nz - 1))
        def _():
            own = pan.at[yh, pl.ds(0, own_rows)]
            remote(own, own, back_s, zy_r.at[0, 0], up).wait_send()

    given = sbuf.at[pl.ds(0, ngroup - 1)]
    remote(given, given, ga_s, ga_r.at[0], {"group": (g + 1) % ngroup}).wait_send()

    @pl.loop(0, EARLY)
    def _(e):
        put(pl.multiple_of(e * 256, 256), 256, e).wait()

    @pl.loop(0, nlate // 2)
    def _(u):
        put(pl.multiple_of(TOP + u * PAIR, 128), PAIR, EARLY + u).wait()


def per_device(ngroup, nblk, front, child_blocks, child_rows, child_cols, child_counts):
    rows = front.shape[1]
    slots = child_blocks.shape[3]
    nstep = FIRST + (rows - TOP) // STEP
    hbm = pl.BlockSpec(memory_space=pltpu.HBM)
    vmem = pl.BlockSpec(memory_space=pltpu.VMEM)
    smem = pl.BlockSpec(memory_space=pltpu.SMEM)
    dma = pltpu.SemaphoreType.DMA
    out, piv = pl.pallas_call(
        functools.partial(kernel, ngroup, nblk, rows),
        out_shape=(
            jax.ShapeDtypeStruct((rows, W), F32),
            jax.ShapeDtypeStruct((1, 2 * W), F32),
        ),
        in_specs=[hbm, hbm, vmem, vmem, smem],
        out_specs=(hbm, vmem),
        scratch_shapes=[
            pltpu.VMEM((rows, W), F32),
            pltpu.VMEM((2, rows + 256, W), F32),
            pltpu.VMEM((ngroup, slots * W + 8, W), F32),
            pltpu.VMEM((ngroup, slots * W + 8, W), F32),
            pltpu.VMEM((ngroup * slots * W, 2 * W), BF16),
            pltpu.VMEM((2 * W, 2 * W), BF16),
            pltpu.VMEM((W, W), F32),
            pltpu.VMEM((W, W), F32),
            dma((2,)), dma((2, nstep)), dma((2,)), dma((2, nstep)),
            dma((2,)), dma((2, nstep)), dma,
            dma, dma((ngroup,)),
            dma, dma, dma, dma((nstep,)),
        ],
        compiler_params=pltpu.CompilerParams(
            collective_id=0, has_side_effects=True, vmem_limit_bytes=56 * 2**20
        ),
        name="extend_and_factor",
    )(
        front[0], child_blocks.reshape(ngroup, slots * W, W), child_rows[0, 0],
        child_cols[0, 0], child_counts.reshape(1, ngroup),
    )
    return out[None], piv


def solution(mesh):
    in_specs = (
        P("group", None, "blk"),
        P("group", "blk", None, None, None, None),
        P("group", "blk", None, None, None),
        P("group", "blk", None, None, None),
        P("group", "blk", None),
    )
    out_specs = (P("group", None, "blk"), P("group", None))
    return jax.shard_map(
        functools.partial(per_device, mesh.shape["group"], mesh.shape["blk"]),
        mesh=mesh, in_specs=in_specs, out_specs=out_specs, check_vma=False,
    )
```
